512 devices in a mesh: face: 4 (over x_hi, core), row: 16 (over z), col: 8 (over y, x_lo).
Axes of the slice: x: 4 (x_hi: 2, x_lo: 2; x = x_hi * 2 + x_lo), y: 4, z: 16, core: 2. Of those that a mesh axis runs over, the one named last changes fastest.
Arguments:
- fields: bfloat16 [12, 512, 8192], P('face', 'row', 'col'), may hold values from -6 to 6
- neighbours: int32 [12, 4, 3], replicated, may hold values from 0 to 11, as said below
- w_enc: bfloat16 [16, 128], replicated, may hold values from -1.5 to 1.5
- depthwise_kernel_first: float32 [3, 3, 128], replicated, may hold values from -2 to 2
- norm_gain_first: float32 [128], replicated, may hold values from 0.1 to 1.9
- expand_weight_first: bfloat16 [128, 512], replicated, may hold values from -0.5 to 0.5
- expand_bias_first: float32 [512], replicated, may hold values from -3 to 3
- contract_weight_first: bfloat16 [512, 128], replicated, may hold values from -0.25 to 0.25
- layer_scale_first: float32 [128], replicated, may hold values from 0.2 to 1
- w_down: bfloat16 [128, 256], replicated, may hold values from -0.5 to 0.5
- depthwise_kernel_second: float32 [3, 3, 256], replicated, may hold values from -2 to 2
- norm_gain_second: float32 [256], replicated, may hold values from 0.1 to 1.9
- expand_weight_second: bfloat16 [256, 1024], replicated, may hold values from -0.375 to 0.375
- expand_bias_second: float32 [1024], replicated, may hold values from -3 to 3
- contract_weight_second: bfloat16 [1024, 256], replicated, may hold values from -0.1875 to 0.1875
- layer_scale_second: float32 [256], replicated, may hold values from 0.2 to 1
Outputs:
- features: bfloat16 [12, 256, 65536], P('face', 'row', 'col')
The draws below stay inside these ranges and needn't reach their ends.
Inputs may be any that keep to these rules, and one draw needn't show every extreme that they name: `neighbours`: faces 3 g, 3 g + 1 and 3 g + 2 form group g. For face f and edge e (0 its first cell row, 1 its last cell row, 2 its first cell column, 3 its last cell column), entry 0 is the face across that edge, which lies in the group of f or in one of the two groups next to it modulo 4; entry 1 is the edge of that face; entry 2 is 1 where position p along the edge meets position 511 - p of the other edge, else 0. Every edge's neighbour names it back.
All inputs are finite; a program needn't handle non-finite values.
Results may differ from the reference program's by a relative error of at most 0.008.
Values may be sent and summed in bfloat16 or wider, within the bound.
No kernel may reach another device: no remote copies, remote signals or barrier semaphores. Data moves between devices by JAX's collectives and lax.ppermute only.
A program may use at most 64 MiB of HBM per device.

```python
import math
import jax
import jax.numpy as jnp
import numpy as np
from jax import lax

CIN = 16
C1 = 128
C2 = 256
HID1 = 512
HID2 = 1024
DILATION_LEVEL1 = 1
DILATION_LEVEL2 = 2
NSIDE = 512


def same_line(first, second):
    return list(first) == list(second)


def orient_tables():
    base = np.arange(9).reshape(3, 3)
    edges = [base[0, :], base[-1, :], base[:, 0], base[:, -1]]
    target = np.zeros((8, 4), np.int32)
    turned = np.zeros((8, 4), np.int32)
    for code in range(8):
        grid = base
        if code & 1:
            grid = grid.T
        if code & 2:
            grid = grid[::-1, :]
        if code & 4:
            grid = grid[:, ::-1]
        stored = [grid[0, :], grid[-1, :], grid[:, 0], grid[:, -1]]
        for slot in range(4):
            for other in range(4):
                if same_line(stored[slot], edges[other]):
                    target[code, slot] = other
                    turned[code, slot] = 0
                if same_line(stored[slot], edges[other][::-1]):
                    target[code, slot] = other
                    turned[code, slot] = 1
    backward = np.zeros((8, 4), np.int32)
    back_turn = np.zeros((8, 4), np.int32)
    for code in range(8):
        for slot in range(4):
            backward[code, target[code, slot]] = slot
            back_turn[code, target[code, slot]] = turned[code, slot]
    return (target, turned, backward, back_turn)


def canonical_links():
    faces_table = np.zeros((12, 4), np.int32)
    edges_table = np.zeros((12, 4), np.int32)
    for group in range(4):
        after = (group + 1) % 4
        before = (group + 3) % 4
        north = 3 * group
        middle = 3 * group + 1
        south = 3 * group + 2
        entries = [(north, 0, 3 * after, 2), (north, 2, 3 * before, 0), (north, 1, 3 * before + 1, 0), (north, 3, middle, 2), (middle, 0, 3 * after, 1), (middle, 2, north, 3), (middle, 3, south, 2), (middle, 1, 3 * before + 2, 0), (south, 2, middle, 3), (south, 0, 3 * after + 1, 1), (south, 1, 3 * before + 2, 3), (south, 3, 3 * after + 2, 1)]
        for source, side, other, other_side in entries:
            faces_table[source, side] = other
            edges_table[source, side] = other_side
    return (faces_table, edges_table)


def draw_neighbours(key, part):
    key = jax.random.fold_in(key, 7)
    codes = jax.random.randint(key, (12,), 0, 8)
    target, turned, backward, back_turn = orient_tables()
    faces_table, edges_table = canonical_links()
    face_ids = jnp.arange(12)[:, None]
    slots = jnp.arange(4)[None, :]
    mine = codes[:, None]
    canon_edge = jnp.asarray(target)[mine, slots]
    first_turn = jnp.asarray(turned)[mine, slots]
    other = jnp.asarray(faces_table)[face_ids, canon_edge]
    other_canon = jnp.asarray(edges_table)[face_ids, canon_edge]
    other_code = codes[other]
    other_edge = jnp.asarray(backward)[other_code, other_canon]
    second_turn = jnp.asarray(back_turn)[other_code, other_canon]
    return jnp.stack([other, other_edge, (first_turn + second_turn) % 2], axis=-1).astype(jnp.int32)


def levels(own_key, shape, split, least, largest):
    level, own = 1.0, jax.random.fold_in(own_key, 6)
    for position, parts in split:
        steps = jnp.exp(jax.random.uniform(jax.random.fold_in(own, position), (parts,), jnp.float32, least / len(split), largest / len(split)))
        level = level * jnp.repeat(steps, shape[position] // parts).reshape([-1 if axis == position else 1 for axis in range(len(shape))])
    return level


def scatter_about(key, extent, width, limit, shards=(), kind=jnp.bfloat16):
    values = jax.random.normal(key, extent, jnp.float32) * width
    if len(shards) > 0:
        values = levels(key, extent, shards, -0.22, 0.18) * values
    return jnp.clip(values, min=-limit, max=limit).astype(kind)


def setup_inputs(seed: int = 0) -> dict:
    seeds = jax.random.split(jax.random.key(seed), 17)
    return {
        "fields": scatter_about(seeds[0], (12, NSIDE, NSIDE * CIN), 1.0, 6.0, ((0, 4), (1, 16), (2, 8))),
        "neighbours": draw_neighbours(jax.random.fold_in(seeds[16], 71), 0),
        "w_enc": scatter_about(seeds[2], (CIN, C1), CIN ** -0.5, 1.5),
        "depthwise_kernel_first": scatter_about(seeds[3], (3, 3, C1), 9 ** -0.5, 2.0, (), jnp.float32),
        "norm_gain_first": jnp.clip(1.0 + 0.18 * jax.random.normal(seeds[4], (C1,), jnp.float32), 0.1, 1.9),
        "expand_weight_first": scatter_about(seeds[5], (C1, HID1), C1 ** -0.5, 0.5),
        "expand_bias_first": scatter_about(seeds[6], (HID1,), 0.5, 3.0, (), jnp.float32),
        "contract_weight_first": scatter_about(seeds[7], (HID1, C1), HID1 ** -0.5, 0.25),
        "layer_scale_first": jnp.clip(jnp.exp(jax.random.uniform(seeds[8], (C1,), jnp.float32, math.log(0.2), math.log(1.0))), 0.2, 1.0),
        "w_down": scatter_about(seeds[9], (C1, C2), C1 ** -0.5, 0.5),
        "depthwise_kernel_second": scatter_about(seeds[10], (3, 3, C2), 9 ** -0.5, 2.0, (), jnp.float32),
        "norm_gain_second": jnp.clip(1.0 + 0.18 * jax.random.normal(seeds[11], (C2,), jnp.float32), 0.1, 1.9),
        "expand_weight_second": scatter_about(seeds[12], (C2, HID2), C2 ** -0.5, 0.375),
        "expand_bias_second": scatter_about(seeds[13], (HID2,), 0.5, 3.0, (), jnp.float32),
        "contract_weight_second": scatter_about(seeds[14], (HID2, C2), HID2 ** -0.5, 0.1875),
        "layer_scale_second": jnp.clip(jnp.exp(jax.random.uniform(seeds[15], (C2,), jnp.float32, math.log(0.2), math.log(1.0))), 0.2, 1.0),
    }


EPSILON = 1e-06

def edge_strips(field, dilation):
    upper = field[:, :dilation]
    lower = jnp.flip(field[:, field.shape[1] - dilation:], axis=1)
    leftmost = jnp.transpose(field[:, :, :dilation], (0, 2, 1, 3))
    rightmost = jnp.transpose(jnp.flip(field[:, :, field.shape[2] - dilation:], axis=2), (0, 2, 1, 3))
    return jnp.stack([upper, lower, leftmost, rightmost], axis=1)

def pad_face(face, bands, dilation):
    channels = face.shape[2]
    upper = jnp.flip(bands[0], axis=0)
    lower = bands[1]
    leftmost = jnp.transpose(jnp.flip(bands[2], axis=0), (1, 0, 2))
    rightmost = jnp.transpose(bands[3], (1, 0, 2))
    middle = jnp.concatenate([leftmost, face, rightmost], axis=1)
    corner = jnp.zeros((dilation, dilation, channels), face.dtype)
    top_rows = jnp.concatenate([corner, upper, corner], axis=1)
    bottom_rows = jnp.concatenate([corner, lower, corner], axis=1)
    return jnp.concatenate([top_rows, middle, bottom_rows], axis=0)

def convnext(padded, field, kernel, gain, w_in, b_in, w_out, scale, dilation):
    height, breadth, channels = field.shape
    mixed = jnp.zeros((height, breadth, channels), jnp.float32)
    for tap_row in range(3):
        for tap_col in range(3):
            window = padded[tap_row * dilation:tap_row * dilation + height, tap_col * dilation:tap_col * dilation + breadth]
            mixed = mixed + window.astype(jnp.float32) * kernel[tap_row, tap_col]
    center = lax.optimization_barrier(jnp.mean(mixed, axis=-1, keepdims=True))
    spread = lax.optimization_barrier(jnp.mean(jnp.square(mixed - center), axis=-1, keepdims=True))
    normed = ((mixed - center) * lax.rsqrt(spread + EPSILON) * gain).astype(jnp.bfloat16)
    hidden = jnp.dot(normed.reshape(-1, channels), w_in, preferred_element_type=jnp.float32) + b_in
    hidden = jax.nn.gelu(hidden, approximate=False).astype(jnp.bfloat16)
    update = jnp.dot(hidden, w_out, preferred_element_type=jnp.float32)
    result = field.reshape(-1, channels).astype(jnp.float32) + scale * update
    return result.astype(jnp.bfloat16).reshape(height, breadth, channels)

def convnext_level_block(field, neighbours, kernel, gain, w_in, b_in, w_out, scale, dilation):
    strips = edge_strips(field, dilation)
    bands = strips[neighbours[:, :, 0], neighbours[:, :, 1]]
    bands = jnp.where(neighbours[:, :, 2][:, :, None, None, None] == 1, jnp.flip(bands, axis=3), bands)

    def one_face(item):
        face, face_bands = item
        return convnext(pad_face(face, face_bands, dilation), face, kernel, gain, w_in, b_in, w_out, scale, dilation)
    return lax.map(one_face, (field, bands))

def reference(fields, neighbours, w_enc, depthwise_kernel_first, norm_gain_first, expand_weight_first, expand_bias_first, contract_weight_first, layer_scale_first, w_down, depthwise_kernel_second, norm_gain_second, expand_weight_second, expand_bias_second, contract_weight_second, layer_scale_second):
    nside = fields.shape[1]
    grid = fields.reshape(12, nside, nside, CIN)

    def encode(face):
        product = jnp.dot(face.reshape(-1, CIN), w_enc, preferred_element_type=jnp.float32)
        return product.astype(jnp.bfloat16).reshape(nside, nside, C1)
    encoder_level_zeroth = lax.map(encode, grid)
    encoder_level_first = convnext_level_block(encoder_level_zeroth, neighbours, depthwise_kernel_first, norm_gain_first, expand_weight_first, expand_bias_first, contract_weight_first, layer_scale_first, DILATION_LEVEL1)
    coarse = nside // 2

    def reduce_face(face):
        pooled = face.astype(jnp.float32).reshape(coarse, 2, coarse, 2, C1).mean(axis=(1, 3)).astype(jnp.bfloat16)
        product = jnp.dot(pooled.reshape(-1, C1), w_down, preferred_element_type=jnp.float32)
        return product.astype(jnp.bfloat16).reshape(coarse, coarse, C2)
    coarse_input = lax.map(reduce_face, encoder_level_first)
    features = convnext_level_block(coarse_input, neighbours, depthwise_kernel_second, norm_gain_second, expand_weight_second, expand_bias_second, contract_weight_second, layer_scale_second, DILATION_LEVEL2)
    return features.reshape(12, coarse, coarse * C2)
```

```python
import functools

import jax
import jax.numpy as jnp
import numpy as np
from jax import lax
from jax.experimental import pallas as pl
from jax.experimental.pallas import tpu as pltpu
from jax.sharding import PartitionSpec as P

CIN = 16
C1 = 128
C2 = 256
HID1 = 512
HID2 = 1024
EPSILON = 1e-06
DEPTH = 5
F32 = jnp.float32
BF16 = jnp.bfloat16

ERF = (7.97827572e-01, 3.64699375e-02, -1.25479103e-04, -3.04667360e-05, 1.11260815e-06)


def upper_windows():
    table = np.zeros((8, 16), np.int32)
    for c in range(8):
        for dest in range(16):
            flipped = 15 - dest
            if dest // 2 == c:
                table[c, dest] = dest % 2
            elif flipped // 2 == c:
                table[c, dest] = flipped % 2
            elif 2 * c + 2 in (dest, flipped):
                table[c, dest] = 1
    return table


UPPER = upper_windows()


def gelu(x):
    square = jnp.minimum(x * x, 36.0)
    poly = ERF[4]
    for coefficient in ERF[3::-1]:
        poly = poly * square + coefficient
    half = 0.5 * x
    return half + half * jnp.tanh(x * poly)


def spots(shape, dim):
    return lax.broadcasted_iota(jnp.int32, shape, dim)


def one_hot(mask):
    return jnp.where(mask, 1.0, 0.0).astype(BF16)


def dot(a, b):
    return jnp.dot(a, b, preferred_element_type=F32)


def route_kernel(nb, pos, recv, own, opp, out, chunks, strip):
    g, r, c = pos[0], pos[1], pos[2]
    outer = jnp.logical_or(r == 0, r == 15)
    side = jnp.logical_or(c == 0, c == 7)
    out[...] = jnp.zeros_like(out)
    chunks[...] = jnp.zeros_like(chunks)

    @pl.when(outer)
    def _():
        mine = jnp.where(r == 0, 0, 1)
        chunks[mine, 8:72, :] = own[...].astype(F32)
        chunks[1 - mine, 8:72, :] = opp[...].astype(F32)

    @pl.when(jnp.logical_not(outer))
    def _():
        flip = 15 - r
        far = jnp.where(
            r // 2 == c,
            r % 2,
            jnp.where(
                flip // 2 == c,
                flip % 2,
                jnp.where(jnp.logical_or(r == 2 * c + 2, flip == 2 * c + 2), 1, 0),
            ),
        )
        start = pl.multiple_of(8 + 16 * far, 8)
        chunks[0, pl.ds(start, 48), :] = recv[0].astype(F32)
        chunks[1, pl.ds(start, 48), :] = recv[15].astype(F32)

    @pl.when(side)
    def _():
        strip[0:8, :] = jnp.zeros((8, 256), F32)
        strip[520:528, :] = jnp.zeros((8, 256), F32)
        for k in range(16):
            strip[8 + 32 * k : 40 + 32 * k, :] = recv[k, 0:32, :].astype(F32)

        @pl.when(jnp.logical_not(outer))
        def _():
            for k, row in ((0, 32), (15, 488)):
                block = recv[k].astype(F32)
                strip[row : row + 8, :] = jnp.where(c == 0, block[0:8], block[40:48])

    def lanes(source_face, dest_face, dest_edge):
        a = spots((256, 256), 0)
        b = spots((256, 256), 1)
        rest = b - 80 * dest_face
        depth = rest // 16
        depth = jnp.where(dest_edge == 2, 4 - depth, depth)
        wanted = 80 * source_face + 16 * depth + rest % 16
        return one_hot(
            jnp.logical_and(jnp.logical_and(rest >= 0, rest < 80), a == wanted)
        )

    def one_strip(k, carry):
        face, edge = k // 4, k % 4
        base = ((3 * g + face) * 4 + edge) * 3
        other, dest_edge, turned = nb[base], nb[base + 1], nb[base + 2]
        dest_group, dest_face = other // 3, other % 3
        along_rows = edge < 2
        dest_rows = dest_edge < 2

        @pl.when(jnp.logical_and(along_rows, jnp.logical_not(dest_rows)))
        def _():
            data = chunks[edge].astype(BF16)
            moved = dot(data, lanes(face, dest_face, dest_edge)).astype(BF16)
            q = 64 * c + spots((48, 80), 1) - 8
            p = jnp.where(turned == 1, 511 - q, q)
            pick = one_hot(p - 32 * r + 8 == spots((48, 80), 0))
            block = dest_group * 8 + jnp.where(dest_edge == 2, 0, 7)
            out[block, 80:128, :] += dot(pick, moved).astype(BF16)

        @pl.when(
            jnp.logical_and(
                jnp.logical_and(along_rows, outer),
                jnp.logical_and(dest_rows, dest_edge == jnp.where(r == 0, 0, 1)),
            )
        )
        def _():
            data = chunks[edge].astype(BF16)
            moved = dot(data, lanes(face, dest_face, dest_edge)).astype(BF16)
            q = 64 * c + spots((80, 80), 1) - 8
            p = jnp.where(turned == 1, 511 - q, q)
            middle = jnp.where(turned == 1, 7 - c, c)
            for shift in (-1, 0, 1):
                target = middle + shift

                @pl.when(jnp.logical_and(target >= 0, target < 8))
                def _():
                    pick = one_hot(p - 64 * target + 8 == spots((80, 80), 0))
                    out[dest_group * 8 + target, 0:80, :] += dot(pick, moved).astype(BF16)

        held = jnp.logical_or(
            jnp.logical_and(edge == 2, c == 0), jnp.logical_and(edge == 3, c == 7)
        )

        @pl.when(jnp.logical_and(held, jnp.logical_not(dest_rows)))
        def _():
            start = pl.multiple_of(32 * jnp.where(turned == 1, 15 - r, r), 8)
            data = strip[pl.ds(start, 48), :].astype(BF16)
            moved = dot(data, lanes(face, dest_face, dest_edge)).astype(BF16)
            x = spots((48, 48), 1)
            pick = one_hot(jnp.where(turned == 1, 47 - x, x) == spots((48, 48), 0))
            block = dest_group * 8 + jnp.where(dest_edge == 2, 0, 7)
            out[block, 80:128, :] += dot(pick, moved).astype(BF16)

        @pl.when(
            jnp.logical_and(
                jnp.logical_and(held, outer),
                jnp.logical_and(dest_rows, dest_edge == jnp.where(r == 0, 0, 1)),
            )
        )
        def _():
            place = lanes(face, dest_face, dest_edge)
            x = spots((80, 80), 1)
            pick = one_hot(jnp.where(turned == 1, 79 - x, x) == spots((80, 80), 0))

            def one_chunk(target, carry):
                start = pl.multiple_of(
                    jnp.where(turned == 1, 448 - 64 * target, 64 * target), 8
                )
                data = strip[pl.ds(start, 80), :].astype(BF16)
                moved = dot(data, place).astype(BF16)
                out[dest_group * 8 + target, 0:80, :] += dot(pick, moved).astype(BF16)
                return carry

            lax.fori_loop(0, 8, one_chunk, 0)

        return carry

    lax.fori_loop(0, 12, one_strip, 0)

    @pl.when(jnp.logical_and(outer, side))
    def _():
        def one_run(k, carry):
            group, rest = k // 12, k % 12
            right, run = rest // 6, rest % 6
            level, dest_face = run // 3, run % 3
            dest_edge = jnp.where(
                level == 0, jnp.where(r == 0, 0, 1), jnp.where(right == 1, 3, 2)
            )
            first = ((3 * group + dest_face) * 4 + dest_edge) * 3
            far = jnp.where(level == 0, right, jnp.where(r == 0, 0, 1))
            edge = nb[first + 1]
            far = jnp.where(nb[first + 2] == 1, 1 - far, far)
            across = jnp.where(edge < 2, 2 + far, far)
            second = (nb[first] * 4 + across) * 3
            edge_far = edge % 2
            source, source_edge = nb[second], nb[second + 1]
            end = jnp.where(nb[second + 2] == 1, 1 - edge_far, edge_far)
            column = jnp.where(
                source_edge == 2, 0, jnp.where(source_edge == 3, 7, jnp.where(end == 0, 0, 7))
            )

            @pl.when(jnp.logical_and(source // 3 == g, column == c))
            def _():
                a = spots((256, 256), 0)
                b = spots((256, 256), 1)
                place = one_hot(
                    jnp.logical_and(b >= 240, a == 80 * (source % 3) + b - 240)
                )
                near = pl.multiple_of(jnp.where(end == 1, 64, 8), 8)
                in_chunk = chunks[jnp.minimum(source_edge, 1), pl.ds(near, 8), :]
                wide = pl.multiple_of(jnp.where(end == 1, 512, 8), 8)
                in_strip = strip[pl.ds(wide, 8), :]
                data = jnp.where(source_edge < 2, in_chunk, in_strip).astype(BF16)
                moved = dot(data, place).astype(BF16)
                x = spots((16, 8), 1)
                order = jnp.where(end == 1, 7 - x, x)
                order = jnp.where(order < DEPTH, order + 8 * (run % 2), -1)
                pick = one_hot(order == spots((16, 8), 0))
                row = pl.multiple_of(16 * (run // 2), 16)
                out[group * 8 + 7 * right, pl.ds(row, 16), :] += dot(pick, moved).astype(BF16)

            return carry

        lax.fori_loop(0, 48, one_run, 0)


def normalise(mixed, gain):
    center = jnp.mean(mixed, axis=-1, keepdims=True)
    apart = mixed - center
    spread = jnp.mean(apart * apart, axis=-1, keepdims=True)
    return (apart * lax.rsqrt(spread + EPSILON) * gain).astype(BF16)


def rounded(x):
    return x.astype(BF16).astype(F32)


def block_kernel(
    nb,
    pos,
    fields,
    above,
    below,
    before,
    after,
    bands,
    enc_cells,
    enc_bands,
    kernel_first,
    gain_first,
    expand_first,
    bias_first,
    contract_first,
    scale_first,
    down,
    kernel_second,
    gain_second,
    expand_second,
    bias_second,
    contract_second,
    scale_second,
    out,
    cells,
    grid,
    banded,
    taps,
    mix,
    rows,
    pooled,
    coarse,
):
    g, r, c = pos[0], pos[1], pos[2]
    top, bottom, left, right = r == 0, r == 15, c == 0, c == 7
    outer = jnp.logical_or(top, bottom)
    side = jnp.logical_or(left, right)
    corner = jnp.logical_and(outer, side)

    @pl.when(jnp.logical_or(outer, side))
    def _():
        def add(k, total):
            return total + bands[k].astype(F32)

        total = lax.fori_loop(0, 32, add, jnp.zeros((128, 256), F32)).astype(BF16)
        for k in range(16):
            banded[k] = rounded(dot(total, enc_bands[:, 128 * k : 128 * k + 128]))

    def band_tap(face, edge, a, b):
        base = ((3 * g + face) * 4 + edge) * 3
        other_edge, turned = nb[base + 1], nb[base + 2]
        down_row, down_col = a - 1, b - 1
        deep = jnp.where(
            edge == 0,
            -down_row,
            jnp.where(edge == 1, down_row, jnp.where(edge == 2, -down_col, down_col)),
        )
        along = jnp.where(edge < 2, down_col, down_row)
        along = jnp.where(turned == 1, -along, along)
        inward = jnp.where(other_edge % 2 == 0, deep, -deep)
        tap_row = jnp.where(other_edge < 2, inward, along)
        tap_col = jnp.where(other_edge < 2, along, inward)
        return kernel_first[pl.ds((tap_row + 1) * 3 + tap_col + 1, 1), :]

    def one_face(i, carry):
        cells[0] = before[i].astype(F32)
        cells[9] = after[i].astype(F32)
        for k in range(8):
            cells[1 + k, 0:8, :] = above[i, :, 128 * k : 128 * k + 128].astype(F32)
            cells[1 + k, 8:40, :] = fields[i, :, 128 * k : 128 * k + 128].astype(F32)
            cells[1 + k, 40:48, :] = below[i, :, 128 * k : 128 * k + 128].astype(F32)

        def encode(k, carry):
            product = rounded(dot(cells[k].astype(BF16), enc_cells[...]))
            for j in range(8):
                grid[8 * k + j] = product[:, 128 * j : 128 * j + 128]
            return carry

        lax.fori_loop(0, 10, encode, 0)

        @pl.when(left)
        def _():
            for k in range(DEPTH):
                grid[3 + k] = banded[5 * i + k, 80:128, :]

        @pl.when(right)
        def _():
            for k in range(DEPTH):
                grid[72 + k] = banded[5 * i + k, 80:128, :]

        @pl.when(outer)
        def _():
            def one_cell(j, carry):
                for k in range(DEPTH):
                    line = banded[5 * i + k, pl.ds(j, 1), :]
                    grid[j, pl.ds(jnp.where(top, 7 - k, 40 + k), 1), :] = line
                return carry

            lax.fori_loop(0, 80, one_cell, 0)

        for a in range(3):
            for b in range(3):
                tap = jnp.broadcast_to(kernel_first[3 * a + b : 3 * a + b + 1, :], (40, 128))
                for kind in range(3):
                    taps[kind, 3 * a + b] = tap

        @pl.when(outer)
        def _():
            edge = jnp.where(top, 0, 1)
            for a in range(3):
                for b in range(3):
                    line = jnp.broadcast_to(band_tap(i, edge, a, b), (4, 128))
                    for kind in range(3):

                        @pl.when(top)
                        def _():
                            taps[kind, 3 * a + b, 0:4, :] = line

                        @pl.when(bottom)
                        def _():
                            taps[kind, 3 * a + b, 36:40, :] = line

        @pl.when(side)
        def _():
            edge = jnp.where(left, 2, 3)
            for a in range(3):
                for b in range(3):
                    line = band_tap(i, edge, a, b)
                    taps[jnp.where(left, 0, 2), 3 * a + b] = jnp.broadcast_to(line, (40, 128))

        def one_chunk(k, carry):
            j0 = 4 + 8 * k
            for half in range(2):
                start = j0 + 4 * half
                place = 2 * k + half
                kind = jnp.where(place == 0, 0, jnp.where(place == 17, 2, 1))
                total = jnp.zeros((4, 40, 128), F32)
                for a in range(3):
                    for b in range(3):
                        window = grid[pl.ds(start + b - 1, 4), 3 + a : 43 + a, :]
                        total = total + window * taps[kind, 3 * a + b][None]
                mix[4 * half : 4 * half + 4] = total

            @pl.when(jnp.logical_and(corner, k == jnp.where(left, 0, 8)))
            def _():
                edge_row = jnp.where(top, 0, 1)
                edge_col = jnp.where(left, 2, 3)
                out_a = jnp.where(top, 0, 2)
                out_b = jnp.where(left, 0, 2)
                row_in, row_out = jnp.where(top, 8, 39), jnp.where(top, 7, 40)
                col_in, col_out = jnp.where(left, 8, 71), jnp.where(left, 7, 72)
                step_row, step_col = jnp.where(top, -1, 1), jnp.where(left, -1, 1)
                row_lines = [-grid[col_out, pl.ds(row_in, 1), :]] + [
                    banded[15, pl.ds(8 * i + d, 1), :] for d in range(DEPTH)
                ]
                col_lines = [-grid[col_in, pl.ds(row_out, 1), :]] + [
                    banded[15, pl.ds(24 + 8 * i + d, 1), :] for d in range(DEPTH)
                ]
                row_taps = [band_tap(i, edge_row, 1 + s * step_row, out_b) for s in (-1, 0, 1)]
                col_taps = [band_tap(i, edge_col, out_a, 1 + s * step_col) for s in (-1, 0, 1)]
                for depth in range(4):
                    extra = sum(row_taps[s] * row_lines[depth + s] for s in range(3))
                    at = (col_in - j0, pl.ds(row_out + depth * step_row - 4, 1))
                    mix[at[0], at[1], :] += extra
                    extra = sum(col_taps[s] * col_lines[depth + s] for s in range(3))
                    at = (col_out + depth * step_col - j0, pl.ds(row_in - 4, 1))
                    mix[at[0], at[1], :] += extra

            normed = normalise(mix[...].reshape(320, C1), gain_first[...])
            hidden = gelu(dot(normed, expand_first[...]) + bias_first[...]).astype(BF16)
            update = dot(hidden, contract_first[...])
            here = grid[pl.ds(j0, 8), 4:44, :].reshape(320, C1)
            rows[...] = rounded(here + scale_first[...] * update).reshape(8, 40, C1)
            paired = rows[:, pl.ds(0, 20, stride=2), :] + rows[:, pl.ds(1, 20, stride=2), :]
            paired = paired.reshape(4, 2, 20, C1)
            pooled[pl.ds(4 * k, 4), 0:20, :] = 0.25 * (paired[:, 0] + paired[:, 1])
            return carry

        lax.fori_loop(0, 9, one_chunk, 0)
        pooled[:, 20:24, :] = jnp.zeros((36, 4, C1), F32)
        product = dot(pooled[...].reshape(36 * 24, C1).astype(BF16), down[...])
        coarse[...] = rounded(product).reshape(36, 24, C2)

        for at_row, row in ((top, 0), (bottom, 18)):
            for at_col, column in ((left, 0), (right, 34)):

                @pl.when(jnp.logical_and(at_row, at_col))
                def _():
                    coarse[column : column + 2, row : row + 2, :] = jnp.zeros((2, 2, C2), F32)

        for part in range(2):
            total = jnp.zeros((16, 16, C2), F32)
            for a in range(3):
                for b in range(3):
                    window = coarse[16 * part + 2 * b : 16 * part + 2 * b + 16, 2 * a : 2 * a + 16, :]
                    total = total + window * kernel_second[3 * a + b : 3 * a + b + 1, :][None]
            normed = normalise(total.reshape(256, C2), gain_second[...])
            hidden = gelu(dot(normed, expand_second[...]) + bias_second[...]).astype(BF16)
            update = dot(hidden, contract_second[...])
            here = coarse[16 * part + 2 : 16 * part + 18, 2:18, :].reshape(256, C2)
            result = (here + scale_second[...] * update).astype(BF16).reshape(16, 16, C2)
            for j in range(16):
                column = (16 * part + j) * C2
                out[i, :, column : column + C2] = result[j]
        return carry

    lax.fori_loop(0, 3, one_face, 0)


def per_device(
    fields,
    neighbours,
    w_enc,
    depthwise_kernel_first,
    norm_gain_first,
    expand_weight_first,
    expand_bias_first,
    contract_weight_first,
    layer_scale_first,
    w_down,
    depthwise_kernel_second,
    norm_gain_second,
    expand_weight_second,
    expand_bias_second,
    contract_weight_second,
    layer_scale_second,
):
    r, c = lax.axis_index("row"), lax.axis_index("col")
    pos = jnp.stack([lax.axis_index("face"), r, c]).astype(jnp.int32)
    links = neighbours.reshape(144)

    lines = jnp.where(r == 15, jnp.flip(fields[:, 27:], axis=1), fields[:, :5])
    lines = lines.reshape(3, 5, 64, CIN).transpose(2, 0, 1, 3).reshape(64, 240)
    lines = jnp.pad(lines, ((0, 0), (0, 16)))
    sides = jnp.where(
        c == 7,
        jnp.flip(fields[:, :, 59 * CIN :].reshape(3, 32, 5, CIN), axis=2),
        fields[:, :, : 5 * CIN].reshape(3, 32, 5, CIN),
    )
    sides = sides.transpose(1, 0, 2, 3).reshape(32, 240)
    sides = jnp.pad(sides, ((0, 16), (0, 16)))
    on_side = jnp.logical_or(c == 0, c == 7)
    outer = jnp.logical_or(r == 0, r == 15)
    nearest = jnp.where(r == 0, sides[24:32], sides[0:8])
    upper = jnp.concatenate(
        [jnp.where(c == 0, nearest, lines[16:24]), lines[24:]], axis=0
    )
    lower = jnp.concatenate(
        [lines[:40], jnp.where(c == 7, nearest, lines[40:48])], axis=0
    )
    chosen = lax.dynamic_index_in_dim(jnp.asarray(UPPER), c, 0, keepdims=False)
    windows = jnp.where((chosen == 1)[:, None, None], upper[None], lower[None])
    inner = np.arange(16)
    inner = jnp.asarray((inner > 0) & (inner < 15))
    use_lines = jnp.logical_and(outer, inner)[:, None, None]
    send = jnp.where(use_lines, windows, sides[None])
    recv = lax.all_to_all(send, "row", 0, 0)
    opposite = lax.ppermute(lines, "row", [(0, 15), (15, 0)])

    above = lax.ppermute(fields[:, 24:], "row", [(k, k + 1) for k in range(15)])
    below = lax.ppermute(fields[:, :8], "row", [(k + 1, k) for k in range(15)])
    first = jnp.concatenate([above[:, :, :128], fields[:, :, :128], below[:, :, :128]], axis=1)
    last = jnp.concatenate([above[:, :, 896:], fields[:, :, 896:], below[:, :, 896:]], axis=1)
    before = lax.ppermute(last, "col", [(k, k + 1) for k in range(7)])
    after = lax.ppermute(first, "col", [(k + 1, k) for k in range(7)])

    smem = pl.BlockSpec(memory_space=pltpu.SMEM)
    vmem = pl.BlockSpec(memory_space=pltpu.VMEM)
    routed = pl.pallas_call(
        route_kernel,
        out_shape=jax.ShapeDtypeStruct((32, 128, 256), BF16),
        in_specs=[smem, smem, vmem, vmem, vmem],
        out_specs=vmem,
        scratch_shapes=[pltpu.VMEM((2, 80, 256), F32), pltpu.VMEM((528, 256), F32)],
        compiler_params=pltpu.CompilerParams(vmem_limit_bytes=32 * 2**20),
        name="route",
    )(links, pos, recv, lines, opposite)
    bands = lax.all_to_all(routed, ("face", "col"), 0, 0)

    enc_cells = jnp.kron(jnp.eye(8, dtype=BF16), w_enc)
    enc_bands = jnp.kron(jnp.eye(16, dtype=BF16), w_enc)
    operands = (
        links,
        pos,
        fields,
        above,
        below,
        before,
        after,
        bands,
        enc_cells,
        enc_bands,
        depthwise_kernel_first.reshape(9, C1),
        norm_gain_first.reshape(1, C1),
        expand_weight_first,
        expand_bias_first.reshape(1, HID1),
        contract_weight_first,
        layer_scale_first.reshape(1, C1),
        w_down,
        depthwise_kernel_second.reshape(9, C2),
        norm_gain_second.reshape(1, C2),
        expand_weight_second,
        expand_bias_second.reshape(1, HID2),
        contract_weight_second,
        layer_scale_second.reshape(1, C2),
    )
    return pl.pallas_call(
        block_kernel,
        out_shape=jax.ShapeDtypeStruct((3, 16, 32 * C2), BF16),
        in_specs=[smem, smem] + [vmem] * (len(operands) - 2),
        out_specs=vmem,
        scratch_shapes=[
            pltpu.VMEM((10, 48, 128), F32),
            pltpu.VMEM((80, 48, 128), F32),
            pltpu.VMEM((16, 128, 128), F32),
            pltpu.VMEM((3, 9, 40, 128), F32),
            pltpu.VMEM((8, 40, 128), F32),
            pltpu.VMEM((8, 40, 128), F32),
            pltpu.VMEM((36, 24, 128), F32),
            pltpu.VMEM((36, 24, 256), F32),
        ],
        compiler_params=pltpu.CompilerParams(vmem_limit_bytes=48 * 2**20),
        name="blocks",
    )(*operands)


def solution(mesh):
    return jax.shard_map(
        per_device,
        mesh=mesh,
        in_specs=(P("face", "row", "col"),) + (P(),) * 15,
        out_specs=P("face", "row", "col"),
        check_vma=False,
    )
```

```python
import jax
import jax.numpy as jnp
from jax import lax
from jax.experimental import pallas as pl
from jax.experimental.pallas import tpu as pltpu
from jax.sharding import PartitionSpec as P

CIN = 16
C1 = 128
C2 = 256
HID1 = 512
HID2 = 1024
EPSILON = 1e-06
DEPTH = 5
F32 = jnp.float32
BF16 = jnp.bfloat16

ERF = (7.97827572e-01, 3.64699375e-02, -1.25479103e-04, -3.04667360e-05, 1.11260815e-06)


def gelu(x):
    x = x.astype(BF16)
    square = jnp.minimum(x * x, BF16(36.0))
    poly = BF16(ERF[4])
    for coefficient in ERF[3::-1]:
        poly = poly * square + BF16(coefficient)
    half = BF16(0.5) * x
    return half + half * jnp.tanh(x * poly)


def spots(shape, dim):
    return lax.broadcasted_iota(jnp.int32, shape, dim)


def one_hot(mask):
    return jnp.where(mask, 1.0, 0.0).astype(BF16)


def third(x):
    return (11 * x) >> 5


def dot(a, b):
    return jnp.dot(a, b, preferred_element_type=F32)


def route_kernel(nb, pos, recv, own, opp, target, chunks, strip, out, sem):
    g, r, c = pos[0], pos[1], pos[2]
    outer = jnp.logical_or(r == 0, r == 15)
    side = jnp.logical_or(c == 0, c == 7)
    out[...] = jnp.zeros_like(out)
    chunks[...] = jnp.zeros_like(chunks)

    @pl.when(outer)
    def _():
        mine = jnp.where(r == 0, 0, 1)
        chunks[mine, 8:72, :] = own[...].astype(F32)
        chunks[1 - mine, 8:72, :] = opp[...].astype(F32)

    @pl.when(jnp.logical_not(outer))
    def _():
        flip = 15 - r
        far = jnp.where(
            r >> 1 == c,
            r & 1,
            jnp.where(
                flip >> 1 == c,
                flip & 1,
                jnp.where(jnp.logical_or(r == 2 * c + 2, flip == 2 * c + 2), 1, 0),
            ),
        )
        start = pl.multiple_of(8 + 16 * far, 8)
        chunks[0, pl.ds(start, 48), :] = recv[0].astype(F32)
        chunks[1, pl.ds(start, 48), :] = recv[15].astype(F32)

    @pl.when(side)
    def _():
        strip[0:8, :] = jnp.zeros((8, 256), F32)
        strip[520:528, :] = jnp.zeros((8, 256), F32)
        for k in range(16):
            strip[8 + 32 * k : 40 + 32 * k, :] = recv[k, 0:32, :].astype(F32)

        @pl.when(jnp.logical_not(outer))
        def _():
            for k, row in ((0, 32), (15, 488)):
                block = recv[k].astype(F32)
                strip[row : row + 8, :] = jnp.where(c == 0, block[0:8], block[40:48])

    def place(data, source_face, dest_face):
        moved = pltpu.roll(data, (80 * (dest_face - source_face) + 256) & 255, 1)
        lane = spots(data.shape, 1) - 80 * dest_face
        inside = jnp.logical_and(lane >= 0, lane < 80)
        return jnp.where(inside, moved, 0.0).astype(BF16)

    def one_strip(k, carry):
        face, edge = k >> 2, k & 3
        base = ((3 * g + face) * 4 + edge) * 3
        other, dest_edge, turned = nb[base], nb[base + 1], nb[base + 2]
        dest_group = third(other)
        dest_face = other - 3 * dest_group
        dest_rows = dest_edge < 2
        to_rows = jnp.logical_and(
            outer, jnp.logical_and(dest_rows, dest_edge == jnp.where(r == 0, 0, 1))
        )
        to_cols = jnp.logical_not(dest_rows)
        block = dest_group * 8 + jnp.where(dest_edge == 2, 0, 7)

        @pl.when(edge < 2)
        def _():
            @pl.when(to_cols)
            def _():
                moved = place(chunks[edge], face, dest_face)
                q = 64 * c + spots((48, 80), 1) - 8
                p = jnp.where(turned == 1, 511 - q, q)
                pick = one_hot(p - 32 * r + 8 == spots((48, 80), 0))
                out[block, 80:128, :] += dot(pick, moved).astype(BF16)

            @pl.when(to_rows)
            def _():
                moved = place(chunks[edge], face, dest_face)
                q = 64 * c + spots((80, 80), 1) - 8
                p = jnp.where(turned == 1, 511 - q, q)
                middle = jnp.where(turned == 1, 7 - c, c)
                for shift in (-1, 0, 1):
                    target = middle + shift

                    @pl.when(jnp.logical_and(target >= 0, target < 8))
                    def _():
                        pick = one_hot(p - 64 * target + 8 == spots((80, 80), 0))
                        out[dest_group * 8 + target, 0:80, :] += dot(pick, moved).astype(BF16)

        @pl.when(jnp.logical_and(edge >= 2, c == jnp.where(edge == 2, 0, 7)))
        def _():
            @pl.when(to_cols)
            def _():
                start = pl.multiple_of(32 * jnp.where(turned == 1, 15 - r, r), 8)
                moved = place(strip[pl.ds(start, 48), :], face, dest_face)
                x = spots((48, 48), 1)
                pick = one_hot(jnp.where(turned == 1, 47 - x, x) == spots((48, 48), 0))
                out[block, 80:128, :] += dot(pick, moved).astype(BF16)

            @pl.when(to_rows)
            def _():
                x = spots((80, 80), 1)
                pick = one_hot(jnp.where(turned == 1, 79 - x, x) == spots((80, 80), 0))
                for target in range(8):
                    start = pl.multiple_of(
                        jnp.where(turned == 1, 448 - 64 * target, 64 * target), 8
                    )
                    moved = place(strip[pl.ds(start, 80), :], face, dest_face)
                    out[dest_group * 8 + target, 0:80, :] += dot(pick, moved).astype(BF16)

        return carry

    lax.fori_loop(0, 12, one_strip, 0)

    @pl.when(jnp.logical_and(outer, side))
    def _():
        def one_run(k, carry):
            face, kind = k >> 2, k & 3
            edge = jnp.where(kind < 2, kind, jnp.where(c == 0, 2, 3))
            end = jnp.where(kind < 2, jnp.where(c == 0, 0, 1), kind & 1)
            first = ((3 * g + face) * 4 + edge) * 3
            between, across = nb[first], nb[first + 1]
            far = jnp.where(nb[first + 2] == 1, 1 - end, end)
            second = (between * 4 + jnp.where(across < 2, 2 + far, far)) * 3
            dest, dest_edge = nb[second], nb[second + 1]
            near = across & 1
            near = jnp.where(nb[second + 2] == 1, 1 - near, near)
            dest_group = third(dest)
            slot = dest - 3 * dest_group + jnp.where(dest_edge < 2, 0, 3)
            dest_row = jnp.where(dest_edge < 2, dest_edge, near)
            dest_col = jnp.where(dest_edge < 2, near, dest_edge - 2)

            @pl.when(dest_row == jnp.where(r == 0, 0, 1))
            def _():
                at_chunk = pl.multiple_of(jnp.where(end == 1, 64, 8), 8)
                at_strip = pl.multiple_of(jnp.where(end == 1, 512, 8), 8)
                data = jnp.where(
                    edge < 2,
                    chunks[jnp.minimum(edge, 1), pl.ds(at_chunk, 8), :],
                    strip[pl.ds(at_strip, 8), :],
                )
                data = pltpu.roll(data, 240 - 80 * face, 1)[:, 128:256]
                data = jnp.where(spots((8, 128), 1) >= 112, data, 0.0)
                data = jnp.concatenate([data, jnp.zeros((8, 128), F32)], axis=0).astype(BF16)
                row = pl.multiple_of(16 * slot, 16)
                out[dest_group * 8 + 7 * dest_col, pl.ds(row, 16), 128:256] += data

            return carry

        lax.fori_loop(0, 12, one_run, 0)

    copy = pltpu.make_async_copy(out, target, sem)
    copy.start()
    copy.wait()


def normalise(mixed, gain):
    center = jnp.mean(mixed, axis=-1, keepdims=True)
    apart = mixed - center
    spread = jnp.mean(apart * apart, axis=-1, keepdims=True)
    return (apart * lax.rsqrt(spread + EPSILON) * gain).astype(BF16)


def rounded(x):
    return x.astype(BF16).astype(F32)


def fetch(sources, targets, sems):
    copies = [
        pltpu.make_async_copy(a, b, sems.at[k]) for k, (a, b) in enumerate(zip(sources, targets))
    ]
    for copy in copies:
        copy.start()
    return copies


def spread(index, above, fields, below, before, after, cells):
    cells[0] = before[index].astype(F32)
    cells[9] = after[index].astype(F32)
    for k in range(8):
        cells[1 + k, 0:8, :] = above[index, :, 128 * k : 128 * k + 128].astype(F32)
        cells[1 + k, 8:40, :] = fields[index, :, 128 * k : 128 * k + 128].astype(F32)
        cells[1 + k, 40:48, :] = below[index, :, 128 * k : 128 * k + 128].astype(F32)


def bulk_kernel(
    pos, fields, above, below, before, after, enc_cells,
    kernel_first, gain_first, expand_first, bias_first, contract_first, scale_first, down,
    kernel_second, gain_second, expand_second, bias_second, contract_second, scale_second,
    out, edge_rows, edge_cols,
    cells, grid, rows, pooled, coarse, *rest,
):
    r, c = pos[1], pos[2]
    sources = (
        kernel_first, gain_first, expand_first, bias_first, contract_first, scale_first, down,
        kernel_second, gain_second, expand_second, bias_second, contract_second, scale_second,
    )
    held, sems = rest[:-1], rest[-1]
    copies = fetch(sources, held, sems)
    (
        kernel_first, gain_first, expand_first, bias_first, contract_first, scale_first, down,
        kernel_second, gain_second, expand_second, bias_second, contract_second, scale_second,
    ) = held
    for copy in copies:
        copy.wait()

    def one_face(i, carry):
        spread(i, above, fields, below, before, after, cells)

        stacked = cells[...].reshape(480, 128).astype(BF16)
        for n in range(4):
            product = rounded(dot(stacked, enc_cells[:, 256 * n : 256 * n + 256]))
            for k in range(10):
                for j in range(2):
                    grid[8 * k + 2 * n + j] = product[48 * k : 48 * k + 48, 128 * j : 128 * j + 128]

        def one_chunk(k, carry):
            j0 = 4 + 8 * k
            total = jnp.zeros((8, 40, 128), F32)
            for a in range(3):
                for b in range(3):
                    window = grid[pl.ds(j0 + b - 1, 8), 3 + a : 43 + a, :]
                    total = total + window * kernel_first[3 * a + b : 3 * a + b + 1, :][None]
            normed = normalise(total.reshape(320, C1), gain_first[...])
            hidden = gelu(dot(normed, expand_first[...]) + bias_first[...]).astype(BF16)
            update = dot(hidden, contract_first[...])
            here = grid[pl.ds(j0, 8), 4:44, :].reshape(320, C1)
            rows[...] = rounded(here + scale_first[...] * update).reshape(8, 40, C1)
            paired = rows[:, pl.ds(0, 20, stride=2), :] + rows[:, pl.ds(1, 20, stride=2), :]
            paired = paired.reshape(4, 2, 20, C1)
            pooled[pl.ds(4 * k, 4), 0:20, :] = 0.25 * (paired[:, 0] + paired[:, 1])
            return carry

        lax.fori_loop(0, 9, one_chunk, 0, unroll=3)
        pooled[:, 20:24, :] = jnp.zeros((36, 4, C1), F32)
        product = dot(pooled[...].reshape(36 * 24, C1).astype(BF16), down[...])
        coarse[...] = rounded(product).reshape(36, 24, C2)

        @pl.when(r == 0)
        def _():
            edge_rows[i] = coarse[:, 0:8, :]

        @pl.when(r == 15)
        def _():
            edge_rows[i, :, 0:7, :] = coarse[:, 13:20, :]

        @pl.when(c == 0)
        def _():
            edge_cols[i] = coarse[0:7]

        @pl.when(c == 7)
        def _():
            edge_cols[i] = coarse[29:36]

        for part in range(2):
            total = jnp.zeros((16, 16, C2), F32)
            for a in range(3):
                for b in range(3):
                    window = coarse[16 * part + 2 * b : 16 * part + 2 * b + 16, 2 * a : 2 * a + 16, :]
                    total = total + window * kernel_second[3 * a + b : 3 * a + b + 1, :][None]
            normed = normalise(total.reshape(256, C2), gain_second[...])
            hidden = gelu(dot(normed, expand_second[...]) + bias_second[...]).astype(BF16)
            update = dot(hidden, contract_second[...])
            here = coarse[16 * part + 2 : 16 * part + 18, 2:18, :].reshape(256, C2)
            result = (here + scale_second[...] * update).astype(BF16).reshape(16, 16, C2)
            for j in range(16):
                column = (16 * part + j) * C2
                out[i, :, column : column + C2] = result[j]
        return carry

    lax.fori_loop(0, 3, one_face, 0)


def edge_kernel(
    nb, pos, bands, fields, above, below, before, after, first_out, edge_rows, edge_cols, enc_cells,
    kernel_first, gain_first, expand_first, bias_first, contract_first, scale_first, down,
    kernel_second, gain_second, expand_second, bias_second, contract_second, scale_second,
    out, *scratch,
):
    r, c = pos[1], pos[2]
    either = jnp.logical_or(
        jnp.logical_or(r == 0, r == 15), jnp.logical_or(c == 0, c == 7)
    )
    held, sems = scratch[-23:-1], scratch[-1]
    sources = (
        fields, above, below, before, after, enc_cells,
        kernel_first, gain_first, expand_first, bias_first, contract_first, scale_first, down,
        kernel_second, edge_rows, edge_cols, gain_second, expand_second, bias_second,
        contract_second, scale_second, first_out,
    )

    @pl.when(jnp.logical_not(either))
    def _():
        copy = pltpu.make_async_copy(first_out, held[21], sems.at[21])
        copy.start()
        copy.wait()

    @pl.when(either)
    def _():
        copies = fetch(sources, held, sems)
        patched(nb, pos, bands, held, copies, *scratch[:-23])

    out[...] = held[21][...]


def patched(
    nb, pos, bands, held, copies,
    cells, grid, side_grid, banded, taps, side_taps, mix, strip, rows, pooled, side_pooled,
    level, side_level, mixed, center, packed, patch,
):
    (
        fields, above, below, before, after, enc_cells,
        kernel_first, gain_first, expand_first, bias_first, contract_first, scale_first, down,
        kernel_second, edge_rows, edge_cols, gain_second, expand_second, bias_second,
        contract_second, scale_second, result,
    ) = held
    g, r, c = pos[0], pos[1], pos[2]
    top, bottom, left, right = r == 0, r == 15, c == 0, c == 7
    outer = jnp.logical_or(top, bottom)
    side = jnp.logical_or(left, right)
    corner = jnp.logical_and(outer, side)
    edge_row, edge_col = jnp.where(top, 0, 1), jnp.where(left, 2, 3)

    def add(k, total):
        return total + bands[k].astype(F32)

    total = lax.fori_loop(0, 32, add, jnp.zeros((128, 256), F32), unroll=4).astype(BF16)
    both = jnp.concatenate([total[:, 0:128], total[:, 128:256]], axis=0)
    for copy in copies[:16]:
        copy.wait()
    for k in range(4):
        product = rounded(dot(both, enc_cells[:, 256 * k : 256 * k + 256]))
        for j in range(2):
            banded[2 * k + j] = product[0:128, 128 * j : 128 * j + 128]
            banded[8 + 2 * k + j] = product[128:256, 128 * j : 128 * j + 128]

    def band_tap(face, edge, a, b):
        base = ((3 * g + face) * 4 + edge) * 3
        other_edge, turned = nb[base + 1], nb[base + 2]
        down_row, down_col = a - 1, b - 1
        deep = jnp.where(
            edge == 0,
            -down_row,
            jnp.where(edge == 1, down_row, jnp.where(edge == 2, -down_col, down_col)),
        )
        along = jnp.where(edge < 2, down_col, down_row)
        along = jnp.where(turned == 1, -along, along)
        inward = jnp.where((other_edge & 1) == 0, deep, -deep)
        tap_row = jnp.where(other_edge < 2, inward, along)
        tap_col = jnp.where(other_edge < 2, along, inward)
        return kernel_first[pl.ds((tap_row + 1) * 3 + tap_col + 1, 1), :]

    def run_end(face, edge, end):
        first = ((3 * g + face) * 4 + edge) * 3
        far = jnp.where(nb[first + 2] == 1, 1 - end, end)
        across = jnp.where(nb[first + 1] < 2, 2 + far, far)
        near = nb[first + 1] & 1
        return jnp.where(nb[(nb[first] * 4 + across) * 3 + 2] == 1, 1 - near, near)

    def block_first(total, here):
        normed = normalise(total, gain_first[...])
        hidden = gelu(dot(normed, expand_first[...]) + bias_first[...]).astype(BF16)
        return rounded(here + scale_first[...] * dot(hidden, contract_first[...]))

    for i in range(3):
        spread(i, above, fields, below, before, after, cells.at[i])

    @pl.when(outer)
    def _():
        low = pl.multiple_of(jnp.where(top, 0, 32), 8)
        data = cells[:, :, pl.ds(low, 16), :].reshape(480, 128).astype(BF16)
        for n in range(4):
            product = rounded(dot(data, enc_cells[:, 256 * n : 256 * n + 256]))
            for i in range(3):
                for k in range(10):
                    for j in range(2):
                        row = 160 * i + 16 * k
                        line = product[row : row + 16, 128 * j : 128 * j + 128]
                        grid[80 * i + 8 * k + 2 * n + j] = line
        flat = grid.reshape(3840, 128)
        for at, first, step in ((top, 7, -1), (bottom, 8, 1)):

            @pl.when(at)
            def _():
                for i in range(3):
                    for k in range(DEPTH):
                        line = banded[5 * i + k, 0:80, :]
                        flat[pl.ds(1280 * i + first + step * k, 80, stride=16), :] = line

        for a in range(3):
            for b in range(3):
                own = jnp.broadcast_to(kernel_first[3 * a + b : 3 * a + b + 1, :], (4, 128))
                for i in range(3):
                    line = jnp.broadcast_to(band_tap(i, edge_row, a, b), (4, 128))
                    taps[9 * i + 3 * a + b, 0:4, :] = jnp.where(top, line, own)
                    taps[9 * i + 3 * a + b, 4:8, :] = jnp.where(top, own, line)

        def one_chunk(k, carry):
            i = (k * 11) >> 5
            j0 = 80 * i + 4 + 24 * (k - 3 * i)
            total = jnp.zeros((24, 8, 128), F32)
            for a in range(3):
                for b in range(3):
                    window = grid[pl.ds(j0 + b - 1, 24), 3 + a : 11 + a, :]
                    total = total + window * taps[9 * i + 3 * a + b][None]
            here = grid[pl.ds(j0, 24), 4:12, :].reshape(192, C1)
            slot = lax.rem(k, 3)
            strip[slot] = block_first(total.reshape(192, C1), here).reshape(24, 8, C1)
            paired = strip[slot, :, pl.ds(0, 4, stride=2), :] + strip[slot, :, pl.ds(1, 4, stride=2), :]
            paired = paired.reshape(12, 2, 4, C1)
            pooled[pl.ds(12 * k, 12), 0:4, :] = 0.25 * (paired[:, 0] + paired[:, 1])
            return carry

        pooled[...] = jnp.zeros_like(pooled)
        lax.fori_loop(0, 9, one_chunk, 0, unroll=3)
        product = rounded(dot(pooled[...].reshape(864, C1).astype(BF16), down[...]))
        product = product.reshape(108, 8, C2)
        level[...] = edge_rows[...].reshape(108, 8, C2)

        @pl.when(top)
        def _():
            level[:, 0:4, :] = product[:, 0:4]

        @pl.when(bottom)
        def _():
            level[:, 3:7, :] = product[:, 0:4]

    @pl.when(side)
    def _():
        group = jnp.where(left, 0, 8)
        data = cells[:, pl.ds(group, 2)].reshape(288, 128).astype(BF16)
        for n in range(4):
            product = rounded(dot(data, enc_cells[:, 256 * n : 256 * n + 256]))
            for i in range(3):
                for k in range(2):
                    for j in range(2):
                        row = 96 * i + 48 * k
                        line = product[row : row + 48, 128 * j : 128 * j + 128]
                        side_grid[16 * i + 8 * k + 2 * n + j] = line
        for i in range(3):
            for k in range(DEPTH):
                j = jnp.where(left, 7 - k, 8 + k)
                side_grid[16 * i + j] = banded[5 * i + k, 80:128, :]

        flat = side_grid.reshape(2304, 128)
        near = pl.multiple_of(jnp.where(left, 0, 64), 8)
        for at, first, step in ((top, 7, -1), (bottom, 40, 1)):

            @pl.when(at)
            def _():
                for i in range(3):
                    for k in range(DEPTH):
                        line = banded[5 * i + k, pl.ds(near, 16), :]
                        flat[pl.ds(768 * i + first + step * k, 16, stride=48), :] = line

        inner = jnp.where(left, 1, 0)
        for a in range(3):
            for b in range(3):
                own = jnp.broadcast_to(kernel_first[3 * a + b : 3 * a + b + 1, :], (40, 128))
                for i in range(3):
                    line = jnp.broadcast_to(band_tap(i, edge_col, a, b), (40, 128))
                    side_taps[i, inner, 3 * a + b] = own
                    side_taps[i, 1 - inner, 3 * a + b] = line

        for at, row in ((top, 0), (bottom, 36)):

            @pl.when(at)
            def _():
                for a in range(3):
                    for b in range(3):
                        for i in range(3):
                            line = jnp.broadcast_to(band_tap(i, edge_row, a, b), (4, 128))
                            side_taps[i, inner, 3 * a + b, row : row + 4, :] = line

        for i in range(3):
            for half in range(2):
                total = jnp.zeros((4, 40, 128), F32)
                for a in range(3):
                    for b in range(3):
                        j = 16 * i + 3 + 4 * half + b
                        window = side_grid[j : j + 4, 3 + a : 43 + a, :]
                        total = total + window * side_taps[i, half, 3 * a + b][None]
                mix[i, 4 * half : 4 * half + 4] = total

        @pl.when(corner)
        def _():
            out_a, out_b = jnp.where(top, 0, 2), jnp.where(left, 0, 2)
            row_in, row_out = jnp.where(top, 8, 39), jnp.where(top, 7, 40)
            col_in, col_out = jnp.where(left, 8, 7), jnp.where(left, 7, 8)
            step_row, step_col = jnp.where(top, -1, 1), jnp.where(left, -1, 1)
            for i in range(3):
                row_end = run_end(i, edge_row, jnp.where(left, 0, 1))
                col_end = run_end(i, edge_col, jnp.where(top, 0, 1))
                row_lines = [-side_grid[16 * i + col_out, pl.ds(row_in, 1), :]] + [
                    banded[15, pl.ds(16 * i + jnp.where(row_end == 1, 7 - d, d), 1), :]
                    for d in range(DEPTH)
                ]
                col_lines = [-side_grid[16 * i + col_in, pl.ds(row_out, 1), :]] + [
                    banded[15, pl.ds(48 + 16 * i + jnp.where(col_end == 1, 7 - d, d), 1), :]
                    for d in range(DEPTH)
                ]
                row_taps = [band_tap(i, edge_row, 1 + s * step_row, out_b) for s in (-1, 0, 1)]
                col_taps = [band_tap(i, edge_col, out_a, 1 + s * step_col) for s in (-1, 0, 1)]
                for depth in range(4):
                    extra = sum(row_taps[s] * row_lines[depth + s] for s in range(3))
                    at = (i, col_in - 4, pl.ds(row_out + depth * step_row - 4, 1))
                    mix[at[0], at[1], at[2], :] += extra
                    extra = sum(col_taps[s] * col_lines[depth + s] for s in range(3))
                    at = (i, col_out + depth * step_col - 4, pl.ds(row_in - 4, 1))
                    mix[at[0], at[1], at[2], :] += extra

        side_pooled[...] = jnp.zeros_like(side_pooled)
        for i in range(3):
            here = side_grid[16 * i + 4 : 16 * i + 12, 4:44, :].reshape(320, C1)
            rows[i] = block_first(mix[i].reshape(320, C1), here).reshape(8, 40, C1)
            paired = rows[i, :, pl.ds(0, 20, stride=2), :] + rows[i, :, pl.ds(1, 20, stride=2), :]
            paired = paired.reshape(4, 2, 20, C1)
            side_pooled[4 * i : 4 * i + 4, 0:20, :] = 0.25 * (paired[:, 0] + paired[:, 1])
        product = rounded(dot(side_pooled[...].reshape(288, C1).astype(BF16), down[...]))
        product = product.reshape(12, 24, C2)
        side_level[...] = edge_cols[...].reshape(21, 24, C2)
        first = jnp.where(left, 0, 29)

        @pl.when(top)
        def _():
            for i in range(3):
                for k in range(7):
                    side_level[7 * i + k, 0:4, :] = level[36 * i + first + k, 0:4, :]

        @pl.when(bottom)
        def _():
            for i in range(3):
                for k in range(7):
                    side_level[7 * i + k, 16:20, :] = level[36 * i + first + k, 3:7, :]

        shift = jnp.where(left, 0, 3)
        dead = jnp.where(left, 0, 5)
        for i in range(3):
            for k in range(4):
                side_level[7 * i + shift + k] = product[4 * i + k]

        for at, row, low in ((top, 0, 0), (bottom, 18, 13)):

            @pl.when(at)
            def _():
                for i in range(3):
                    for k in range(2):
                        side_level[7 * i + dead + k, row : row + 2, :] = jnp.zeros((2, C2), F32)
                    for k in range(7):
                        line = side_level[7 * i + k, low : low + 7, :]
                        level[36 * i + first + k, 0:7, :] = line

    mixed[...] = jnp.zeros_like(mixed)
    center[...] = jnp.zeros_like(center)

    @pl.when(outer)
    def _():
        for i in range(3):
            total = jnp.zeros((32, 3, C2), F32)
            for a in range(3):
                for b in range(3):
                    first = 36 * i + 2 * b
                    window = level[first : first + 32, 2 * a : 2 * a + 3, :]
                    total = total + window * kernel_second[3 * a + b : 3 * a + b + 1, :][None]
            here = level[36 * i + 2 : 36 * i + 34, 2:5, :]
            for j in range(32):
                row = 96 * i + 3 * j
                mixed[row : row + 3, :] = total[j]
                center[row : row + 3, :] = here[j]

    @pl.when(side)
    def _():
        for i in range(3):
            total = jnp.zeros((3, 16, C2), F32)
            for a in range(3):
                for b in range(3):
                    first = 7 * i + 2 * b
                    window = side_level[first : first + 3, 2 * a : 2 * a + 16, :]
                    total = total + window * kernel_second[3 * a + b : 3 * a + b + 1, :][None]
            row = 288 + 48 * i
            mixed[row : row + 48, :] = total.reshape(48, C2)
            center[row : row + 48, :] = side_level[7 * i + 2 : 7 * i + 5, 2:18, :].reshape(48, C2)

    for copy in copies[16:]:
        copy.wait()
    normed = normalise(mixed[...], gain_second[...])
    hidden = gelu(dot(normed, expand_second[...]) + bias_second[...]).astype(BF16)
    center[...] = center[...] + scale_second[...] * dot(hidden, contract_second[...])

    for at, row in ((top, 0), (bottom, 13)):

        @pl.when(at)
        def _():
            for i in range(3):
                patch[...] = result[i].astype(F32)
                for j in range(32):
                    line = center[96 * i + 3 * j : 96 * i + 3 * j + 3, :]
                    patch[row : row + 3, C2 * j : C2 * j + C2] = line
                result[i] = patch[...].astype(BF16)

    for at, col in ((left, 0), (right, 29)):

        @pl.when(at)
        def _():
            for i in range(3):
                for j in range(3):
                    row = 288 + 48 * i + 16 * j
                    lane = C2 * (col + j)
                    result[i, :, lane : lane + C2] = center[row : row + 16, :].astype(BF16)


SMEM = pl.BlockSpec(memory_space=pltpu.SMEM)
WHOLE = pl.BlockSpec(memory_space=pltpu.VMEM)
FAR = pl.BlockSpec(memory_space=pltpu.HBM)

LIMIT = 56 * 2**20


def held_copies(weights):
    held = [pltpu.VMEM(w.shape, w.dtype) for w in weights]
    return held + [pltpu.SemaphoreType.DMA((len(weights),))]


def route(links, pos, recv, lines, opposite):
    return pl.pallas_call(
        route_kernel,
        out_shape=jax.ShapeDtypeStruct((32, 128, 256), BF16),
        in_specs=[SMEM, SMEM, WHOLE, WHOLE, WHOLE],
        out_specs=FAR,
        scratch_shapes=[
            pltpu.VMEM((2, 80, 256), F32),
            pltpu.VMEM((528, 256), F32),
            pltpu.VMEM((32, 128, 256), BF16),
            pltpu.SemaphoreType.DMA,
        ],
        compiler_params=pltpu.CompilerParams(vmem_limit_bytes=LIMIT),
        name="route",
    )(links, pos, recv, lines, opposite)


def bulk(pos, halos, enc_cells, weights):
    return pl.pallas_call(
        bulk_kernel,
        out_shape=(
            jax.ShapeDtypeStruct((3, 16, 32 * C2), BF16),
            jax.ShapeDtypeStruct((3, 36, 8, C2), F32),
            jax.ShapeDtypeStruct((3, 7, 24, C2), F32),
        ),
        in_specs=[SMEM] + [WHOLE] * 6 + [FAR] * len(weights),
        out_specs=(WHOLE, WHOLE, WHOLE),
        scratch_shapes=[
            pltpu.VMEM((10, 48, 128), F32),
            pltpu.VMEM((80, 48, 128), F32),
            pltpu.VMEM((8, 40, 128), F32),
            pltpu.VMEM((36, 24, 128), F32),
            pltpu.VMEM((36, 24, 256), F32),
        ]
        + held_copies(weights),
        compiler_params=pltpu.CompilerParams(vmem_limit_bytes=LIMIT),
        cost_estimate=pl.CostEstimate(
            flops=5 * 10**9, bytes_accessed=4 * 10**6, transcendentals=6 * 10**6
        ),
        name="bulk",
    )(pos, *halos, enc_cells, *weights)


def edges(links, pos, halos, bands, first_out, edge_rows, edge_cols, enc_cells, weights):
    sources = (*halos, enc_cells, *weights[:8], edge_rows, edge_cols, *weights[8:], first_out)
    operands = (*halos, first_out, edge_rows, edge_cols, enc_cells, *weights)
    return pl.pallas_call(
        edge_kernel,
        out_shape=jax.ShapeDtypeStruct((3, 16, 32 * C2), BF16),
        in_specs=[SMEM, SMEM, WHOLE] + [FAR] * len(operands),
        out_specs=WHOLE,
        scratch_shapes=[
            pltpu.VMEM((3, 10, 48, 128), F32),
            pltpu.VMEM((240, 16, 128), F32),
            pltpu.VMEM((48, 48, 128), F32),
            pltpu.VMEM((16, 128, 128), F32),
            pltpu.VMEM((27, 8, 128), F32),
            pltpu.VMEM((3, 2, 9, 40, 128), F32),
            pltpu.VMEM((3, 8, 40, 128), F32),
            pltpu.VMEM((3, 24, 8, 128), F32),
            pltpu.VMEM((3, 8, 40, 128), F32),
            pltpu.VMEM((108, 8, 128), F32),
            pltpu.VMEM((12, 24, 128), F32),
            pltpu.VMEM((108, 8, 256), F32),
            pltpu.VMEM((21, 24, 256), F32),
            pltpu.VMEM((432, 256), F32),
            pltpu.VMEM((432, 256), F32),
            pltpu.VMEM((8, 128), F32),
            pltpu.VMEM((16, 32 * C2), F32),
        ]
        + held_copies(sources),
        compiler_params=pltpu.CompilerParams(vmem_limit_bytes=LIMIT),
        name="edges",
    )(links, pos, bands, *operands)


def as_lines(rows):
    lines = rows.reshape(3, DEPTH, 64, CIN).transpose(2, 0, 1, 3).reshape(64, 240)
    return jnp.pad(lines, ((0, 0), (0, 16)))


def per_device(
    fields,
    neighbours,
    w_enc,
    depthwise_kernel_first,
    norm_gain_first,
    expand_weight_first,
    expand_bias_first,
    contract_weight_first,
    layer_scale_first,
    w_down,
    depthwise_kernel_second,
    norm_gain_second,
    expand_weight_second,
    expand_bias_second,
    contract_weight_second,
    layer_scale_second,
):
    r, c = lax.axis_index("row"), lax.axis_index("col")
    pos = jnp.stack([lax.axis_index("face"), r, c]).astype(jnp.int32)
    links = neighbours.reshape(144)

    lines = jnp.where(r == 15, jnp.flip(fields[:, 27:], axis=1), fields[:, :5])
    lines = as_lines(lines)
    sides = jnp.where(
        c == 7,
        jnp.flip(fields[:, :, 59 * CIN :].reshape(3, 32, 5, CIN), axis=2),
        fields[:, :, : 5 * CIN].reshape(3, 32, 5, CIN),
    )
    sides = sides.transpose(1, 0, 2, 3).reshape(32, 240)
    sides = jnp.pad(sides, ((0, 16), (0, 16)))
    outer = jnp.logical_or(r == 0, r == 15)
    nearest = jnp.where(r == 0, sides[24:32], sides[0:8])
    upper = jnp.concatenate([jnp.where(c == 0, nearest, lines[16:24]), lines[24:]], axis=0)
    lower = jnp.concatenate([lines[:40], jnp.where(c == 7, nearest, lines[40:48])], axis=0)
    dest = lax.broadcasted_iota(jnp.int32, (16, 48, 256), 0)
    far = jnp.where(
        dest >> 1 == c,
        dest & 1,
        jnp.where(
            (15 - dest) >> 1 == c,
            (15 - dest) & 1,
            jnp.where((dest == 2 * c + 2) | (15 - dest == 2 * c + 2), 1, 0),
        ),
    )
    use_lines = jnp.logical_and(outer, (dest > 0) & (dest < 15))
    send = jnp.where(use_lines, jnp.where(far == 1, upper[None], lower[None]), sides[None])
    above = lax.ppermute(fields[:, 24:], "row", [(k, (k + 1) % 16) for k in range(16)])
    below = lax.ppermute(fields[:, :8], "row", [((k + 1) % 16, k) for k in range(16)])
    send, above, below = lax.optimization_barrier((send, above, below))
    recv = lax.all_to_all(send, "row", 0, 0)

    opposite = as_lines(jnp.where(r == 0, jnp.flip(above[:, 3:], axis=1), below[:, :5]))
    first = jnp.concatenate([above[:, :, :128], fields[:, :, :128], below[:, :, :128]], axis=1)
    last = jnp.concatenate([above[:, :, 896:], fields[:, :, 896:], below[:, :, 896:]], axis=1)
    before = lax.ppermute(last, "col", [(k, k + 1) for k in range(7)])
    after = lax.ppermute(first, "col", [(k + 1, k) for k in range(7)])

    recv, before, after = lax.optimization_barrier((recv, before, after))

    routed = route(links, pos, recv, lines, opposite)
    bands = lax.all_to_all(routed, ("face", "col"), 0, 0)

    enc_cells = jnp.kron(jnp.eye(8, dtype=BF16), w_enc)
    weights = (
        depthwise_kernel_first.reshape(9, C1),
        norm_gain_first.reshape(1, C1),
        expand_weight_first,
        expand_bias_first.reshape(1, HID1),
        contract_weight_first,
        layer_scale_first.reshape(1, C1),
        w_down,
        depthwise_kernel_second.reshape(9, C2),
        norm_gain_second.reshape(1, C2),
        expand_weight_second,
        expand_bias_second.reshape(1, HID2),
        contract_weight_second,
        layer_scale_second.reshape(1, C2),
    )
    halos = (fields, above, below, before, after)
    first_out, edge_rows, edge_cols = bulk(pos, halos, enc_cells, weights)
    return edges(links, pos, halos, bands, first_out, edge_rows, edge_cols, enc_cells, weights)


def solution(mesh):
    return jax.shard_map(
        per_device,
        mesh=mesh,
        in_specs=(P("face", "row", "col"),) + (P(),) * 15,
        out_specs=P("face", "row", "col"),
        check_vma=False,
    )
```

```python
import jax
import jax.numpy as jnp
from jax import lax
from jax.experimental import pallas as pl
from jax.experimental.pallas import tpu as pltpu
from jax.sharding import PartitionSpec as P

CIN = 16
C1 = 128
C2 = 256
HID1 = 512
HID2 = 1024
EPSILON = 1e-06
DEPTH = 5
F32 = jnp.float32
BF16 = jnp.bfloat16

ERF = (7.97507541e-01, 3.70060348e-02, -3.51598854e-04)


def gelu(x):
    x = x.astype(BF16)
    square = jnp.minimum(x * x, BF16(36.0))
    poly = BF16(ERF[-1])
    for coefficient in ERF[-2::-1]:
        poly = poly * square + BF16(coefficient)
    half = BF16(0.5) * x
    return half + half * jnp.tanh(x * poly)


def spots(shape, dim):
    return lax.broadcasted_iota(jnp.int32, shape, dim)


def one_hot(mask):
    return jnp.where(mask, 1.0, 0.0).astype(BF16)


def third(x):
    return (11 * x) >> 5


def dot(a, b):
    return jnp.dot(a, b, preferred_element_type=F32)


def strip_kernel(pos, fields, send, lines):
    r, c = pos[1], pos[2]
    lane = spots((1024, 256), 1) & 15
    spread_out = one_hot((spots((1024, 256), 0) & 15) == lane)
    own_cell = (spots((64, 1024), 1) >> 4) == spots((64, 1024), 0)
    parts = []
    for i in range(3):
        near, far = fields[i, 0:16, :].astype(F32), fields[i, 16:32, :].astype(F32)
        for d in range(DEPTH):
            line = jnp.where(r == 15, far[15 - d : 16 - d], near[d : d + 1])
            parts.append(jnp.where(own_cell, line, 0.0).astype(BF16))
    product = dot(jnp.concatenate(parts, axis=0), spread_out)
    place = spots((64, 256), 1) >> 4
    along = jnp.zeros((64, 256), F32)
    for k in range(15):
        along = jnp.where(place == k, product[64 * k : 64 * k + 64], along)
    down = jnp.zeros((32, 256), F32)
    a, b = spots((128, 256), 0), spots((128, 256), 1)
    for i in range(3):
        data = jnp.where(c == 7, fields[i, :, 896:1024].astype(F32), fields[i, :, 0:128].astype(F32))
        depth = (b >> 4) - 5 * i
        depth = jnp.where(jnp.logical_and(depth >= 0, depth < DEPTH), depth, 99)
        cell = jnp.where(c == 7, 7 - depth, depth)
        pick = jnp.logical_and((a >> 4) == cell, (a & 15) == (b & 15))
        down = down + dot(data.astype(BF16), one_hot(pick))
    lines[...] = along.astype(BF16)
    nearest = jnp.where(r == 0, down[24:32], down[0:8])
    upper = jnp.concatenate([jnp.where(c == 0, nearest, along[16:24]), along[24:]], axis=0)
    lower = jnp.concatenate([along[:40], jnp.where(c == 7, nearest, along[40:48])], axis=0)
    upper, lower = upper.astype(BF16), lower.astype(BF16)
    wide = jnp.concatenate([down, jnp.zeros((16, 256), F32)], axis=0).astype(BF16)
    outer = jnp.logical_or(r == 0, r == 15)
    for k in range(16):
        flip = 15 - k
        far = jnp.where(
            c == k >> 1,
            k & 1,
            jnp.where(
                c == flip >> 1,
                flip & 1,
                jnp.where(jnp.logical_or(2 * c + 2 == k, 2 * c + 2 == flip), 1, 0),
            ),
        )
        if 0 < k < 15:
            send[k] = jnp.where(outer, jnp.where(far == 1, upper, lower), wide)
        else:
            send[k] = wide


def route_kernel(nb, pos, recv, own, opp, target, chunks, strip, out, sem):
    g, r, c = pos[0], pos[1], pos[2]
    outer = jnp.logical_or(r == 0, r == 15)
    side = jnp.logical_or(c == 0, c == 7)
    out[...] = jnp.zeros_like(out)
    chunks[...] = jnp.zeros_like(chunks)

    @pl.when(outer)
    def _():
        mine = jnp.where(r == 0, 0, 1)
        chunks[mine, 8:72, :] = own[...].astype(F32)
        chunks[1 - mine, 8:72, :] = opp[...].astype(F32)

    @pl.when(jnp.logical_not(outer))
    def _():
        flip = 15 - r
        far = jnp.where(
            r >> 1 == c,
            r & 1,
            jnp.where(
                flip >> 1 == c,
                flip & 1,
                jnp.where(jnp.logical_or(r == 2 * c + 2, flip == 2 * c + 2), 1, 0),
            ),
        )
        start = pl.multiple_of(8 + 16 * far, 8)
        chunks[0, pl.ds(start, 48), :] = recv[0].astype(F32)
        chunks[1, pl.ds(start, 48), :] = recv[15].astype(F32)

    @pl.when(side)
    def _():
        strip[0:8, :] = jnp.zeros((8, 256), F32)
        strip[520:528, :] = jnp.zeros((8, 256), F32)
        for k in range(16):
            strip[8 + 32 * k : 40 + 32 * k, :] = recv[k, 0:32, :].astype(F32)

        @pl.when(jnp.logical_not(outer))
        def _():
            for k, row in ((0, 32), (15, 488)):
                block = recv[k].astype(F32)
                strip[row : row + 8, :] = jnp.where(c == 0, block[0:8], block[40:48])

    def place(data, source_face, dest_face):
        moved = pltpu.roll(data, (80 * (dest_face - source_face) + 256) & 255, 1)
        lane = spots(data.shape, 1) - 80 * dest_face
        inside = jnp.logical_and(lane >= 0, lane < 80)
        return jnp.where(inside, moved, 0.0).astype(BF16)

    def one_strip(k, carry):
        face, edge = k >> 2, k & 3
        base = ((3 * g + face) * 4 + edge) * 3
        other, dest_edge, turned = nb[base], nb[base + 1], nb[base + 2]
        dest_group = third(other)
        dest_face = other - 3 * dest_group
        dest_rows = dest_edge < 2
        to_rows = jnp.logical_and(
            outer, jnp.logical_and(dest_rows, dest_edge == jnp.where(r == 0, 0, 1))
        )
        to_cols = jnp.logical_not(dest_rows)
        block = dest_group * 8 + jnp.where(dest_edge == 2, 0, 7)
        lower = jnp.where(r == 15, 5, 0)
        line = spots((48, 80), 0) - lower

        @pl.when(edge < 2)
        def _():
            @pl.when(to_cols)
            def _():
                moved = place(chunks[edge], face, dest_face)
                q = 64 * c + spots((48, 80), 1) - 8
                p = jnp.where(turned == 1, 511 - q, q)
                pick = one_hot(jnp.logical_and(p - 32 * r + 8 == line, line >= 3))
                out[block, 64:112, :] += dot(pick, moved).astype(BF16)

            @pl.when(to_rows)
            def _():
                moved = place(chunks[edge], face, dest_face)
                q = 64 * c + spots((80, 80), 1) - 8
                p = jnp.where(turned == 1, 511 - q, q)
                middle = jnp.where(turned == 1, 7 - c, c)
                for shift in (-1, 0, 1):
                    target = middle + shift

                    @pl.when(jnp.logical_and(target >= 0, target < 8))
                    def _():
                        lead = jnp.where(target == 0, 0, 8)
                        seen = p - 64 * target + lead
                        kept = seen < jnp.where(target == 0, 72, 80)
                        pick = one_hot(jnp.logical_and(kept, seen == spots((80, 80), 0)))
                        out[dest_group * 8 + target, 0:80, :] += dot(pick, moved).astype(BF16)

        @pl.when(jnp.logical_and(edge >= 2, c == jnp.where(edge == 2, 0, 7)))
        def _():
            @pl.when(to_cols)
            def _():
                start = pl.multiple_of(32 * jnp.where(turned == 1, 15 - r, r), 8)
                moved = place(strip[pl.ds(start, 48), :], face, dest_face)
                x = spots((48, 48), 1)
                line = spots((48, 48), 0) - lower
                pick = one_hot(jnp.logical_and(jnp.where(turned == 1, 47 - x, x) == line, line >= 3))
                out[block, 64:112, :] += dot(pick, moved).astype(BF16)

            @pl.when(to_rows)
            def _():
                x = spots((80, 80), 1)
                pick = one_hot(jnp.where(turned == 1, 79 - x, x) == spots((80, 80), 0))
                for target in range(8):
                    start = pl.multiple_of(
                        jnp.where(turned == 1, 448 - 64 * target, 64 * target), 8
                    )
                    moved = place(strip[pl.ds(start, 80), :], face, dest_face)
                    chosen = dot(pick, moved)
                    if target == 0:
                        chosen = jnp.concatenate([chosen[8:], jnp.zeros((8, 256), F32)], axis=0)
                    out[dest_group * 8 + target, 0:80, :] += chosen.astype(BF16)

        return carry

    lax.fori_loop(0, 12, one_strip, 0)

    @pl.when(jnp.logical_and(outer, side))
    def _():
        def one_run(k, carry):
            face, kind = k >> 2, k & 3
            edge = jnp.where(kind < 2, kind, jnp.where(c == 0, 2, 3))
            end = jnp.where(kind < 2, jnp.where(c == 0, 0, 1), kind & 1)
            first = ((3 * g + face) * 4 + edge) * 3
            between, across = nb[first], nb[first + 1]
            far = jnp.where(nb[first + 2] == 1, 1 - end, end)
            second = (between * 4 + jnp.where(across < 2, 2 + far, far)) * 3
            dest, dest_edge = nb[second], nb[second + 1]
            near = across & 1
            near = jnp.where(nb[second + 2] == 1, 1 - near, near)
            dest_group = third(dest)
            slot = dest - 3 * dest_group + jnp.where(dest_edge < 2, 0, 3)
            dest_row = jnp.where(dest_edge < 2, dest_edge, near)
            dest_col = jnp.where(dest_edge < 2, near, dest_edge - 2)

            @pl.when(dest_row == jnp.where(r == 0, 0, 1))
            def _():
                at_chunk = pl.multiple_of(jnp.where(end == 1, 64, 8), 8)
                at_strip = pl.multiple_of(jnp.where(end == 1, 512, 8), 8)
                data = jnp.where(
                    edge < 2,
                    chunks[jnp.minimum(edge, 1), pl.ds(at_chunk, 8), :],
                    strip[pl.ds(at_strip, 8), :],
                )
                data = pltpu.roll(data, 240 - 80 * face, 1)[:, 128:256]
                data = jnp.where(spots((8, 128), 1) >= 112, data, 0.0)
                data = jnp.concatenate([data, jnp.zeros((8, 128), F32)], axis=0).astype(BF16)
                row = pl.multiple_of(16 * slot, 16)
                out[dest_group * 8 + 7 * dest_col, pl.ds(row, 16), 128:256] += data

            return carry

        lax.fori_loop(0, 12, one_run, 0)

    copy = pltpu.make_async_copy(out, target, sem)
    copy.start()
    copy.wait()


def normalise(mixed, gain):
    center = jnp.mean(mixed, axis=-1, keepdims=True)
    apart = mixed - center
    spread = jnp.mean(apart * apart, axis=-1, keepdims=True)
    return (apart * lax.rsqrt(spread + EPSILON) * gain).astype(BF16)


def rounded(x):
    return x.astype(BF16).astype(F32)


def fetch(sources, targets, sems):
    copies = [
        pltpu.make_async_copy(a, b, sems.at[k]) for k, (a, b) in enumerate(zip(sources, targets))
    ]
    for copy in copies:
        copy.start()
    return copies


def spread(index, above, fields, below, before, after, cells):
    cells[0, 8:40, :] = before[index].astype(F32)
    cells[9, 8:40, :] = after[index].astype(F32)
    for k in range(8):
        cells[1 + k, 8:40, :] = fields[index, :, 128 * k : 128 * k + 128].astype(F32)
    for k in range(10):
        cells[k, 0:8, :] = above[index, :, 128 * k : 128 * k + 128].astype(F32)
        cells[k, 40:48, :] = below[index, :, 128 * k : 128 * k + 128].astype(F32)


def bulk_kernel(
    pos, fields, above, below, before, after, enc_cells,
    kernel_first, gain_first, expand_first, bias_first, contract_first, scale_first, down,
    kernel_second, gain_second, expand_second, bias_second, contract_second, scale_second,
    out, edge_rows, edge_cols,
    cells, grid, rows, pooled, coarse, result, *rest,
):
    r, c = pos[1], pos[2]
    sources = (
        fields, above, below, before, after, enc_cells,
        kernel_first, gain_first, expand_first, bias_first, contract_first, scale_first, down,
        kernel_second, gain_second, expand_second, bias_second, contract_second, scale_second,
    )
    held, sems, leave = rest[:-2], rest[-2], rest[-1]
    copies = fetch(sources, held, sems)
    (
        fields, above, below, before, after, enc_cells,
        kernel_first, gain_first, expand_first, bias_first, contract_first, scale_first, down,
        kernel_second, gain_second, expand_second, bias_second, contract_second, scale_second,
    ) = held
    for copy in copies[:6]:
        copy.wait()

    def encode(i, carry):
        spread(i, above, fields, below, before, after, cells)
        stacked = cells[...].reshape(480, 128).astype(BF16)
        for n in range(4):
            product = rounded(dot(stacked, enc_cells[:, 256 * n : 256 * n + 256]))
            for k in range(10):
                for j in range(2):
                    line = product[48 * k : 48 * k + 48, 128 * j : 128 * j + 128]
                    grid[80 * i + 8 * k + 2 * n + j] = line
        return carry

    lax.fori_loop(0, 3, encode, 0)
    for copy in copies[6:13]:
        copy.wait()

    def one_face(i, carry):
        def one_chunk(k, carry):
            j0 = 80 * i + 4 + 8 * k
            total = jnp.zeros((8, 40, 128), F32)
            for a in range(3):
                for b in range(3):
                    window = grid[pl.ds(j0 + b - 1, 8), 3 + a : 43 + a, :]
                    total = total + window * kernel_first[3 * a + b : 3 * a + b + 1, :][None]
            normed = normalise(total.reshape(320, C1), gain_first[...])
            hidden = gelu(dot(normed, expand_first[...]) + bias_first[...]).astype(BF16)
            update = dot(hidden, contract_first[...])
            here = grid[pl.ds(j0, 8), 4:44, :].reshape(320, C1)
            rows[...] = rounded(here + scale_first[...] * update).reshape(8, 40, C1)
            paired = rows[:, pl.ds(0, 20, stride=2), :] + rows[:, pl.ds(1, 20, stride=2), :]
            paired = paired.reshape(4, 2, 20, C1)
            pooled[pl.ds(4 * k, 4), 0:20, :] = 0.25 * (paired[:, 0] + paired[:, 1])
            return carry

        lax.fori_loop(0, 9, one_chunk, 0, unroll=9)
        pooled[:, 20:24, :] = jnp.zeros((36, 4, C1), F32)
        product = dot(pooled[...].reshape(36 * 24, C1).astype(BF16), down[...])
        coarse[i] = rounded(product).reshape(36, 24, C2)
        return carry

    lax.fori_loop(0, 3, one_face, 0)
    for copy in copies[13:]:
        copy.wait()

    def at_edges(act):
        for index, (at, source, target) in enumerate(
            (
                (r == 0, coarse.at[:, :, 0:8], edge_rows),
                (r == 15, coarse.at[:, :, 12:20], edge_rows),
                (c == 0, coarse.at[:, 0:7], edge_cols),
                (c == 7, coarse.at[:, 29:36], edge_cols),
            )
        ):

            @pl.when(at)
            def _():
                act(pltpu.make_async_copy(source, target, leave.at[3 + index]))

    at_edges(lambda copy: copy.start())

    def one_part(k, carry):
        i, part = k >> 1, k & 1
        first = 16 * part
        total = jnp.zeros((16, 16, C2), F32)
        for a in range(3):
            for b in range(3):
                window = coarse[i, pl.ds(first + 2 * b, 16), 2 * a : 2 * a + 16, :]
                total = total + window * kernel_second[3 * a + b : 3 * a + b + 1, :][None]
        normed = normalise(total.reshape(256, C2), gain_second[...])
        hidden = gelu(dot(normed, expand_second[...]) + bias_second[...]).astype(BF16)
        update = dot(hidden, contract_second[...])
        here = coarse[i, pl.ds(first + 2, 16), 2:18, :].reshape(256, C2)
        made = (here + scale_second[...] * update).astype(BF16).reshape(16, 16, C2)
        for j in range(16):
            lane = pl.multiple_of((first + j) * C2, C2)
            result[i, :, pl.ds(lane, C2)] = made[j]
        return carry

    for i in range(3):
        lax.fori_loop(2 * i, 2 * i + 2, one_part, 0, unroll=2)
        pltpu.make_async_copy(result.at[i], out.at[i], leave.at[i]).start()
    for i in range(3):
        pltpu.make_async_copy(result.at[i], out.at[i], leave.at[i]).wait()
    at_edges(lambda copy: copy.wait())


def edge_kernel(
    nb, pos, bands, fields, above, below, before, after, first_out, edge_rows, edge_cols, enc_cells,
    kernel_first, gain_first, expand_first, bias_first, contract_first, scale_first, down,
    kernel_second, gain_second, expand_second, bias_second, contract_second, scale_second,
    out, *scratch,
):
    r, c = pos[1], pos[2]
    either = jnp.logical_or(
        jnp.logical_or(r == 0, r == 15), jnp.logical_or(c == 0, c == 7)
    )
    held, sems = scratch[-24:-1], scratch[-1]
    sources = (
        bands, enc_cells, fields, above, below, before, after,
        kernel_first, gain_first, expand_first, bias_first, contract_first, scale_first, down,
        kernel_second, edge_rows, edge_cols, gain_second, expand_second, bias_second,
        contract_second, scale_second, first_out,
    )

    @pl.when(either)
    def _():
        copies = fetch(sources, held, sems)
        patched(nb, pos, held, copies, out, sems, *scratch[:-24])


def patched(
    nb, pos, held, copies, out, sems,
    cells, grid, side_grid, banded, taps, side_taps, mix, strip, rows, pooled, side_pooled,
    level, side_level, mixed, center, packed, patch,
):
    (
        bands, enc_cells, fields, above, below, before, after,
        kernel_first, gain_first, expand_first, bias_first, contract_first, scale_first, down,
        kernel_second, edge_rows, edge_cols, gain_second, expand_second, bias_second,
        contract_second, scale_second, result,
    ) = held
    g, r, c = pos[0], pos[1], pos[2]
    top, bottom, left, right = r == 0, r == 15, c == 0, c == 7
    outer = jnp.logical_or(top, bottom)
    side = jnp.logical_or(left, right)
    corner = jnp.logical_and(outer, side)
    edge_row, edge_col = jnp.where(top, 0, 1), jnp.where(left, 2, 3)

    def add(k, total):
        return total + bands[k]

    copies[0].wait()
    total = lax.fori_loop(0, 32, add, jnp.zeros((112, 256), BF16), unroll=8)
    both = jnp.concatenate([total[:, 0:128], total[:, 128:256]], axis=0)
    copies[1].wait()
    for k in range(4):
        product = rounded(dot(both, enc_cells[:, 256 * k : 256 * k + 256]))
        for j in range(2):
            banded[2 * k + j, 0:112, :] = product[0:112, 128 * j : 128 * j + 128]
            banded[8 + 2 * k + j, 0:112, :] = product[112:224, 128 * j : 128 * j + 128]
    banded[:, 112:120, :] = jnp.zeros((16, 8, 128), F32)
    none = jnp.zeros((8, 128), F32)

    def row_band(k):
        body = banded[k, 0:80, :]
        shifted = jnp.concatenate([none, body[0:72]], axis=0)
        return jnp.where(left, shifted, jnp.concatenate([body[0:72], jnp.where(right, none, body[72:80])], axis=0))

    def row_band_end(k):
        at_left = jnp.concatenate([none, banded[k, 0:8, :]], axis=0)
        return jnp.where(left, at_left, jnp.concatenate([banded[k, 64:72, :], none], axis=0))

    def col_band(k):
        return jnp.where(bottom, banded[k, 69:117, :], banded[k, 64:112, :])

    def band_tap(face, edge, a, b):
        base = ((3 * g + face) * 4 + edge) * 3
        other_edge, turned = nb[base + 1], nb[base + 2]
        down_row, down_col = a - 1, b - 1
        deep = jnp.where(
            edge == 0,
            -down_row,
            jnp.where(edge == 1, down_row, jnp.where(edge == 2, -down_col, down_col)),
        )
        along = jnp.where(edge < 2, down_col, down_row)
        along = jnp.where(turned == 1, -along, along)
        inward = jnp.where((other_edge & 1) == 0, deep, -deep)
        tap_row = jnp.where(other_edge < 2, inward, along)
        tap_col = jnp.where(other_edge < 2, along, inward)
        return kernel_first[pl.ds((tap_row + 1) * 3 + tap_col + 1, 1), :]

    def run_end(face, edge, end):
        first = ((3 * g + face) * 4 + edge) * 3
        far = jnp.where(nb[first + 2] == 1, 1 - end, end)
        across = jnp.where(nb[first + 1] < 2, 2 + far, far)
        near = nb[first + 1] & 1
        return jnp.where(nb[(nb[first] * 4 + across) * 3 + 2] == 1, 1 - near, near)

    def block_first(total, here):
        normed = normalise(total, gain_first[...])
        hidden = gelu(dot(normed, expand_first[...]) + bias_first[...]).astype(BF16)
        return rounded(here + scale_first[...] * dot(hidden, contract_first[...]))

    for copy in copies[2:14]:
        copy.wait()
    for i in range(3):
        spread(i, above, fields, below, before, after, cells.at[i])

    @pl.when(outer)
    def _():
        low = pl.multiple_of(jnp.where(top, 0, 32), 8)
        data = cells[:, :, pl.ds(low, 16), :].reshape(480, 128).astype(BF16)
        for n in range(4):
            product = rounded(dot(data, enc_cells[:, 256 * n : 256 * n + 256]))
            for i in range(3):
                for k in range(10):
                    for j in range(2):
                        row = 160 * i + 16 * k
                        line = product[row : row + 16, 128 * j : 128 * j + 128]
                        grid[80 * i + 8 * k + 2 * n + j] = line
        flat = grid.reshape(3840, 128)
        for at, first, step in ((top, 7, -1), (bottom, 8, 1)):

            @pl.when(at)
            def _():
                for i in range(3):
                    for k in range(DEPTH):
                        line = row_band(5 * i + k)
                        flat[pl.ds(1280 * i + first + step * k, 80, stride=16), :] = line

        for a in range(3):
            for b in range(3):
                own = jnp.broadcast_to(kernel_first[3 * a + b : 3 * a + b + 1, :], (4, 128))
                for i in range(3):
                    line = jnp.broadcast_to(band_tap(i, edge_row, a, b), (4, 128))
                    taps[9 * i + 3 * a + b, 0:4, :] = jnp.where(top, line, own)
                    taps[9 * i + 3 * a + b, 4:8, :] = jnp.where(top, own, line)

        def one_chunk(k, carry):
            i = (k * 11) >> 5
            j0 = 80 * i + 4 + 24 * (k - 3 * i)
            total = jnp.zeros((24, 8, 128), F32)
            for a in range(3):
                for b in range(3):
                    window = grid[pl.ds(j0 + b - 1, 24), 3 + a : 11 + a, :]
                    total = total + window * taps[9 * i + 3 * a + b][None]
            here = grid[pl.ds(j0, 24), 4:12, :].reshape(192, C1)
            slot = lax.rem(k, 3)
            strip[slot] = block_first(total.reshape(192, C1), here).reshape(24, 8, C1)
            paired = strip[slot, :, pl.ds(0, 4, stride=2), :] + strip[slot, :, pl.ds(1, 4, stride=2), :]
            paired = paired.reshape(12, 2, 4, C1)
            pooled[pl.ds(12 * k, 12), 0:4, :] = 0.25 * (paired[:, 0] + paired[:, 1])
            return carry

        pooled[...] = jnp.zeros_like(pooled)
        lax.fori_loop(0, 9, one_chunk, 0, unroll=9)
    for copy in copies[14:17]:
        copy.wait()

    @pl.when(outer)
    def _():
        product = rounded(dot(pooled[...].reshape(864, C1).astype(BF16), down[...]))
        product = product.reshape(108, 8, C2)
        whole = edge_rows[...].reshape(108, 8, C2)
        level[...] = jnp.where(top, whole, jnp.concatenate([whole[:, 1:], whole[:, :1]], axis=1))

        @pl.when(top)
        def _():
            level[:, 0:4, :] = product[:, 0:4]

        @pl.when(bottom)
        def _():
            level[:, 3:7, :] = product[:, 0:4]

    @pl.when(side)
    def _():
        group = jnp.where(left, 0, 8)
        data = cells[:, pl.ds(group, 2)].reshape(288, 128).astype(BF16)
        for n in range(4):
            product = rounded(dot(data, enc_cells[:, 256 * n : 256 * n + 256]))
            for i in range(3):
                for k in range(2):
                    for j in range(2):
                        row = 96 * i + 48 * k
                        line = product[row : row + 48, 128 * j : 128 * j + 128]
                        side_grid[16 * i + 8 * k + 2 * n + j] = line
        for i in range(3):
            for k in range(DEPTH):
                j = jnp.where(left, 7 - k, 8 + k)
                side_grid[16 * i + j] = col_band(5 * i + k)

        flat = side_grid.reshape(2304, 128)
        for at, first, step in ((top, 7, -1), (bottom, 40, 1)):

            @pl.when(at)
            def _():
                for i in range(3):
                    for k in range(DEPTH):
                        line = row_band_end(5 * i + k)
                        flat[pl.ds(768 * i + first + step * k, 16, stride=48), :] = line

        inner = jnp.where(left, 1, 0)
        for a in range(3):
            for b in range(3):
                own = jnp.broadcast_to(kernel_first[3 * a + b : 3 * a + b + 1, :], (40, 128))
                for i in range(3):
                    line = jnp.broadcast_to(band_tap(i, edge_col, a, b), (40, 128))
                    side_taps[i, inner, 3 * a + b] = own
                    side_taps[i, 1 - inner, 3 * a + b] = line

        for at, row in ((top, 0), (bottom, 36)):

            @pl.when(at)
            def _():
                for a in range(3):
                    for b in range(3):
                        for i in range(3):
                            line = jnp.broadcast_to(band_tap(i, edge_row, a, b), (4, 128))
                            side_taps[i, inner, 3 * a + b, row : row + 4, :] = line

        for i in range(3):
            for half in range(2):
                total = jnp.zeros((4, 40, 128), F32)
                for a in range(3):
                    for b in range(3):
                        j = 16 * i + 3 + 4 * half + b
                        window = side_grid[j : j + 4, 3 + a : 43 + a, :]
                        total = total + window * side_taps[i, half, 3 * a + b][None]
                mix[i, 4 * half : 4 * half + 4] = total

        @pl.when(corner)
        def _():
            out_a, out_b = jnp.where(top, 0, 2), jnp.where(left, 0, 2)
            row_in, row_out = jnp.where(top, 8, 39), jnp.where(top, 7, 40)
            col_in, col_out = jnp.where(left, 8, 7), jnp.where(left, 7, 8)
            step_row, step_col = jnp.where(top, -1, 1), jnp.where(left, -1, 1)
            for i in range(3):
                row_end = run_end(i, edge_row, jnp.where(left, 0, 1))
                col_end = run_end(i, edge_col, jnp.where(top, 0, 1))
                row_lines = [-side_grid[16 * i + col_out, pl.ds(row_in, 1), :]] + [
                    banded[15, pl.ds(16 * i + jnp.where(row_end == 1, 7 - d, d), 1), :]
                    for d in range(DEPTH)
                ]
                col_lines = [-side_grid[16 * i + col_in, pl.ds(row_out, 1), :]] + [
                    banded[15, pl.ds(48 + 16 * i + jnp.where(col_end == 1, 7 - d, d), 1), :]
                    for d in range(DEPTH)
                ]
                row_taps = [band_tap(i, edge_row, 1 + s * step_row, out_b) for s in (-1, 0, 1)]
                col_taps = [band_tap(i, edge_col, out_a, 1 + s * step_col) for s in (-1, 0, 1)]
                for depth in range(4):
                    extra = sum(row_taps[s] * row_lines[depth + s] for s in range(3))
                    at = (i, col_in - 4, pl.ds(row_out + depth * step_row - 4, 1))
                    mix[at[0], at[1], at[2], :] += extra
                    extra = sum(col_taps[s] * col_lines[depth + s] for s in range(3))
                    at = (i, col_out + depth * step_col - 4, pl.ds(row_in - 4, 1))
                    mix[at[0], at[1], at[2], :] += extra

        side_pooled[...] = jnp.zeros_like(side_pooled)
        for i in range(3):
            here = side_grid[16 * i + 4 : 16 * i + 12, 4:44, :].reshape(320, C1)
            rows[i] = block_first(mix[i].reshape(320, C1), here).reshape(8, 40, C1)
            paired = rows[i, :, pl.ds(0, 20, stride=2), :] + rows[i, :, pl.ds(1, 20, stride=2), :]
            paired = paired.reshape(4, 2, 20, C1)
            side_pooled[4 * i : 4 * i + 4, 0:20, :] = 0.25 * (paired[:, 0] + paired[:, 1])
        product = rounded(dot(side_pooled[...].reshape(288, C1).astype(BF16), down[...]))
        product = product.reshape(12, 24, C2)
        side_level[...] = edge_cols[...].reshape(21, 24, C2)
        first = jnp.where(left, 0, 29)

        @pl.when(top)
        def _():
            for i in range(3):
                for k in range(7):
                    side_level[7 * i + k, 0:4, :] = level[36 * i + first + k, 0:4, :]

        @pl.when(bottom)
        def _():
            for i in range(3):
                for k in range(7):
                    side_level[7 * i + k, 16:20, :] = level[36 * i + first + k, 3:7, :]

        shift = jnp.where(left, 0, 3)
        dead = jnp.where(left, 0, 5)
        for i in range(3):
            for k in range(4):
                side_level[7 * i + shift + k] = product[4 * i + k]

        for at, row, low in ((top, 0, 0), (bottom, 18, 13)):

            @pl.when(at)
            def _():
                for i in range(3):
                    for k in range(2):
                        side_level[7 * i + dead + k, row : row + 2, :] = jnp.zeros((2, C2), F32)
                    for k in range(7):
                        line = side_level[7 * i + k, low : low + 7, :]
                        level[36 * i + first + k, 0:7, :] = line

    mixed[...] = jnp.zeros_like(mixed)
    center[...] = jnp.zeros_like(center)

    @pl.when(outer)
    def _():
        for i in range(3):
            total = jnp.zeros((32, 3, C2), F32)
            for a in range(3):
                for b in range(3):
                    first = 36 * i + 2 * b
                    window = level[first : first + 32, 2 * a : 2 * a + 3, :]
                    total = total + window * kernel_second[3 * a + b : 3 * a + b + 1, :][None]
            here = level[36 * i + 2 : 36 * i + 34, 2:5, :]
            for j in range(32):
                row = 96 * i + 3 * j
                mixed[row : row + 3, :] = total[j]
                center[row : row + 3, :] = here[j]

    @pl.when(side)
    def _():
        for i in range(3):
            total = jnp.zeros((3, 16, C2), F32)
            for a in range(3):
                for b in range(3):
                    first = 7 * i + 2 * b
                    window = side_level[first : first + 3, 2 * a : 2 * a + 16, :]
                    total = total + window * kernel_second[3 * a + b : 3 * a + b + 1, :][None]
            row = 288 + 48 * i
            mixed[row : row + 48, :] = total.reshape(48, C2)
            center[row : row + 48, :] = side_level[7 * i + 2 : 7 * i + 5, 2:18, :].reshape(48, C2)

    for copy in copies[17:]:
        copy.wait()
    normed = normalise(mixed[...], gain_second[...])
    hidden = gelu(dot(normed, expand_second[...]) + bias_second[...]).astype(BF16)
    center[...] = center[...] + scale_second[...] * dot(hidden, contract_second[...])

    for i in range(3):
        for at, row in ((top, 0), (bottom, 13)):

            @pl.when(at)
            def _():
                patch[...] = result[i].astype(F32)
                for j in range(32):
                    line = center[96 * i + 3 * j : 96 * i + 3 * j + 3, :]
                    patch[row : row + 3, C2 * j : C2 * j + C2] = line
                result[i] = patch[...].astype(BF16)

        for at, col in ((left, 0), (right, 29)):

            @pl.when(at)
            def _():
                for j in range(3):
                    row = 288 + 48 * i + 16 * j
                    lane = C2 * (col + j)
                    result[i, :, lane : lane + C2] = center[row : row + 16, :].astype(BF16)

        pltpu.make_async_copy(result.at[i], out.at[i], sems.at[i]).start()
    for i in range(3):
        pltpu.make_async_copy(result.at[i], out.at[i], sems.at[i]).wait()


SMEM = pl.BlockSpec(memory_space=pltpu.SMEM)
WHOLE = pl.BlockSpec(memory_space=pltpu.VMEM)
FAR = pl.BlockSpec(memory_space=pltpu.HBM)

LIMIT = 56 * 2**20


def held_copies(weights):
    held = [pltpu.VMEM(w.shape, w.dtype) for w in weights]
    return held + [pltpu.SemaphoreType.DMA((len(weights),))]


def strips(pos, fields):
    return pl.pallas_call(
        strip_kernel,
        out_shape=(
            jax.ShapeDtypeStruct((16, 48, 256), BF16),
            jax.ShapeDtypeStruct((64, 256), BF16),
        ),
        in_specs=[SMEM, WHOLE],
        out_specs=(WHOLE, WHOLE),
        compiler_params=pltpu.CompilerParams(vmem_limit_bytes=24 * 2**20),
        name="strips",
    )(pos, fields)


def route(links, pos, recv, lines, opposite):
    return pl.pallas_call(
        route_kernel,
        out_shape=jax.ShapeDtypeStruct((32, 112, 256), BF16),
        in_specs=[SMEM, SMEM, WHOLE, WHOLE, WHOLE],
        out_specs=FAR,
        scratch_shapes=[
            pltpu.VMEM((2, 80, 256), F32),
            pltpu.VMEM((528, 256), F32),
            pltpu.VMEM((32, 112, 256), BF16),
            pltpu.SemaphoreType.DMA,
        ],
        compiler_params=pltpu.CompilerParams(vmem_limit_bytes=16 * 2**20),
        cost_estimate=pl.CostEstimate(
            flops=10**9, bytes_accessed=4 * 10**6, transcendentals=0
        ),
        name="route",
    )(links, pos, recv, lines, opposite)


def bulk(pos, halos, enc_cells, weights):
    operands = (*halos, enc_cells, *weights)
    return pl.pallas_call(
        bulk_kernel,
        out_shape=(
            jax.ShapeDtypeStruct((3, 16, 32 * C2), BF16),
            jax.ShapeDtypeStruct((3, 36, 8, C2), F32),
            jax.ShapeDtypeStruct((3, 7, 24, C2), F32),
        ),
        in_specs=[SMEM] + [FAR] * len(operands),
        out_specs=(FAR, FAR, FAR),
        scratch_shapes=[
            pltpu.VMEM((10, 48, 128), F32),
            pltpu.VMEM((240, 48, 128), F32),
            pltpu.VMEM((8, 40, 128), F32),
            pltpu.VMEM((36, 24, 128), F32),
            pltpu.VMEM((3, 36, 24, 256), F32),
            pltpu.VMEM((3, 16, 32 * C2), BF16),
        ]
        + held_copies(operands)
        + [pltpu.SemaphoreType.DMA((7,))],
        compiler_params=pltpu.CompilerParams(vmem_limit_bytes=LIMIT),
        cost_estimate=pl.CostEstimate(
            flops=5 * 10**9, bytes_accessed=4 * 10**6, transcendentals=6 * 10**6
        ),
        name="bulk",
    )(pos, *operands)


def edges(links, pos, halos, bands, first_out, edge_rows, edge_cols, enc_cells, weights):
    sources = (bands, enc_cells, *halos, *weights[:8], edge_rows, edge_cols, *weights[8:], first_out)
    operands = (bands, *halos, first_out, edge_rows, edge_cols, enc_cells, *weights)
    return pl.pallas_call(
        edge_kernel,
        out_shape=jax.ShapeDtypeStruct((3, 16, 32 * C2), BF16),
        in_specs=[SMEM, SMEM] + [FAR] * len(operands),
        out_specs=FAR,
        input_output_aliases={2 + len(halos) + 1: 0},
        scratch_shapes=[
            pltpu.VMEM((3, 10, 48, 128), F32),
            pltpu.VMEM((240, 16, 128), F32),
            pltpu.VMEM((48, 48, 128), F32),
            pltpu.VMEM((16, 120, 128), F32),
            pltpu.VMEM((27, 8, 128), F32),
            pltpu.VMEM((3, 2, 9, 40, 128), F32),
            pltpu.VMEM((3, 8, 40, 128), F32),
            pltpu.VMEM((3, 24, 8, 128), F32),
            pltpu.VMEM((3, 8, 40, 128), F32),
            pltpu.VMEM((108, 8, 128), F32),
            pltpu.VMEM((12, 24, 128), F32),
            pltpu.VMEM((108, 8, 256), F32),
            pltpu.VMEM((21, 24, 256), F32),
            pltpu.VMEM((432, 256), F32),
            pltpu.VMEM((432, 256), F32),
            pltpu.VMEM((8, 128), F32),
            pltpu.VMEM((16, 32 * C2), F32),
        ]
        + held_copies(sources),
        compiler_params=pltpu.CompilerParams(vmem_limit_bytes=LIMIT),
        name="edges",
    )(links, pos, *operands)


def per_device(
    fields,
    neighbours,
    w_enc,
    depthwise_kernel_first,
    norm_gain_first,
    expand_weight_first,
    expand_bias_first,
    contract_weight_first,
    layer_scale_first,
    w_down,
    depthwise_kernel_second,
    norm_gain_second,
    expand_weight_second,
    expand_bias_second,
    contract_weight_second,
    layer_scale_second,
):
    r, c = lax.axis_index("row"), lax.axis_index("col")
    pos = jnp.stack([lax.axis_index("face"), r, c]).astype(jnp.int32)
    links = neighbours.reshape(144)

    send, lines = strips(pos, fields)
    recv = lax.all_to_all(send, "row", 0, 0)
    opposite = lax.ppermute(lines, "row", [(0, 15), (15, 0)])

    before = lax.ppermute(fields[:, :, 896:], "col", [(k, k + 1) for k in range(7)])
    after = lax.ppermute(fields[:, :, :128], "col", [(k + 1, k) for k in range(7)])
    wide = jnp.concatenate([before, fields, after], axis=2)
    above = lax.ppermute(wide[:, 24:], "row", [(k, k + 1) for k in range(15)])
    below = lax.ppermute(wide[:, :8], "row", [(k + 1, k) for k in range(15)])

    routed = route(links, pos, recv, lines, opposite)
    routed, above, below = lax.optimization_barrier((routed, above, below))
    bands = lax.all_to_all(routed, ("face", "col"), 0, 0)

    enc_cells = jnp.kron(jnp.eye(8, dtype=BF16), w_enc)
    weights = (
        depthwise_kernel_first.reshape(9, C1),
        norm_gain_first.reshape(1, C1),
        expand_weight_first,
        expand_bias_first.reshape(1, HID1),
        contract_weight_first,
        layer_scale_first.reshape(1, C1),
        w_down,
        depthwise_kernel_second.reshape(9, C2),
        norm_gain_second.reshape(1, C2),
        expand_weight_second,
        expand_bias_second.reshape(1, HID2),
        contract_weight_second,
        layer_scale_second.reshape(1, C2),
    )
    halos = (fields, above, below, before, after)
    first_out, edge_rows, edge_cols = bulk(pos, halos, enc_cells, weights)
    return edges(links, pos, halos, bands, first_out, edge_rows, edge_cols, enc_cells, weights)


def solution(mesh):
    return jax.shard_map(
        per_device,
        mesh=mesh,
        in_specs=(P("face", "row", "col"),) + (P(),) * 15,
        out_specs=P("face", "row", "col"),
        check_vma=False,
    )
```

```python
import jax
import jax.numpy as jnp
from jax import lax
from jax.experimental import pallas as pl
from jax.experimental.pallas import tpu as pltpu
from jax.sharding import PartitionSpec as P

CIN = 16
C1 = 128
C2 = 256
HID1 = 512
HID2 = 1024
EPSILON = 1e-06
DEPTH = 5
F32 = jnp.float32
BF16 = jnp.bfloat16

ERF = (7.97507541e-01, 3.70060348e-02, -3.51598854e-04)


def gelu(x):
    x = x.astype(BF16)
    square = jnp.minimum(x * x, BF16(36.0))
    poly = BF16(ERF[-1])
    for coefficient in ERF[-2::-1]:
        poly = poly * square + BF16(coefficient)
    half = BF16(0.5) * x
    return half + half * jnp.tanh(x * poly)


def spots(shape, dim):
    return lax.broadcasted_iota(jnp.int32, shape, dim)


def one_hot(mask):
    return jnp.where(mask, 1.0, 0.0).astype(BF16)


def third(x):
    return (11 * x) >> 5


def dot(a, b):
    return jnp.dot(a, b, preferred_element_type=F32)


def strip_kernel(pos, fields, send, lines):
    r, c = pos[1], pos[2]
    lane = spots((1024, 256), 1) & 15
    spread_out = one_hot((spots((1024, 256), 0) & 15) == lane)
    own_cell = (spots((64, 1024), 1) >> 4) == spots((64, 1024), 0)
    parts = []
    for i in range(3):
        near, far = fields[i, 0:16, :].astype(F32), fields[i, 16:32, :].astype(F32)
        for d in range(DEPTH):
            line = jnp.where(r == 15, far[15 - d : 16 - d], near[d : d + 1])
            parts.append(jnp.where(own_cell, line, 0.0).astype(BF16))
    product = dot(jnp.concatenate(parts, axis=0), spread_out)
    place = spots((64, 256), 1) >> 4
    along = jnp.zeros((64, 256), F32)
    for k in range(15):
        along = jnp.where(place == k, product[64 * k : 64 * k + 64], along)
    down = jnp.zeros((32, 256), F32)
    a, b = spots((128, 256), 0), spots((128, 256), 1)
    for i in range(3):
        data = jnp.where(c == 7, fields[i, :, 896:1024].astype(F32), fields[i, :, 0:128].astype(F32))
        depth = (b >> 4) - 5 * i
        depth = jnp.where(jnp.logical_and(depth >= 0, depth < DEPTH), depth, 99)
        cell = jnp.where(c == 7, 7 - depth, depth)
        pick = jnp.logical_and((a >> 4) == cell, (a & 15) == (b & 15))
        down = down + dot(data.astype(BF16), one_hot(pick))
    lines[...] = along.astype(BF16)
    nearest = jnp.where(r == 0, down[24:32], down[0:8])
    upper = jnp.concatenate([jnp.where(c == 0, nearest, along[16:24]), along[24:]], axis=0)
    lower = jnp.concatenate([along[:40], jnp.where(c == 7, nearest, along[40:48])], axis=0)
    upper, lower = upper.astype(BF16), lower.astype(BF16)
    wide = jnp.concatenate([down, jnp.zeros((16, 256), F32)], axis=0).astype(BF16)
    outer = jnp.logical_or(r == 0, r == 15)
    for k in range(16):
        flip = 15 - k
        far = jnp.where(
            c == k >> 1,
            k & 1,
            jnp.where(
                c == flip >> 1,
                flip & 1,
                jnp.where(jnp.logical_or(2 * c + 2 == k, 2 * c + 2 == flip), 1, 0),
            ),
        )
        if 0 < k < 15:
            send[k] = jnp.where(outer, jnp.where(far == 1, upper, lower), wide)
        else:
            send[k] = wide


def route_kernel(nb, pos, recv, own, opp, target, chunks, strip, out, sem):
    g, r, c = pos[0], pos[1], pos[2]
    outer = jnp.logical_or(r == 0, r == 15)
    side = jnp.logical_or(c == 0, c == 7)
    out[...] = jnp.zeros_like(out)
    chunks[...] = jnp.zeros_like(chunks)

    @pl.when(outer)
    def _():
        mine = jnp.where(r == 0, 0, 1)
        chunks[mine, 8:72, :] = own[...].astype(F32)
        chunks[1 - mine, 8:72, :] = opp[...].astype(F32)

    @pl.when(jnp.logical_not(outer))
    def _():
        flip = 15 - r
        far = jnp.where(
            r >> 1 == c,
            r & 1,
            jnp.where(
                flip >> 1 == c,
                flip & 1,
                jnp.where(jnp.logical_or(r == 2 * c + 2, flip == 2 * c + 2), 1, 0),
            ),
        )
        start = pl.multiple_of(8 + 16 * far, 8)
        chunks[0, pl.ds(start, 48), :] = recv[0].astype(F32)
        chunks[1, pl.ds(start, 48), :] = recv[15].astype(F32)

    @pl.when(side)
    def _():
        strip[0:8, :] = jnp.zeros((8, 256), F32)
        strip[520:528, :] = jnp.zeros((8, 256), F32)
        for k in range(16):
            strip[8 + 32 * k : 40 + 32 * k, :] = recv[k, 0:32, :].astype(F32)

        @pl.when(jnp.logical_not(outer))
        def _():
            for k, row in ((0, 32), (15, 488)):
                block = recv[k].astype(F32)
                strip[row : row + 8, :] = jnp.where(c == 0, block[0:8], block[40:48])

    def place(data, source_face, dest_face):
        moved = pltpu.roll(data, (80 * (dest_face - source_face) + 256) & 255, 1)
        lane = spots(data.shape, 1) - 80 * dest_face
        inside = jnp.logical_and(lane >= 0, lane < 80)
        return jnp.where(inside, moved, 0.0).astype(BF16)

    def one_strip(k, carry):
        face, edge = k >> 2, k & 3
        base = ((3 * g + face) * 4 + edge) * 3
        other, dest_edge, turned = nb[base], nb[base + 1], nb[base + 2]
        dest_group = third(other)
        dest_face = other - 3 * dest_group
        dest_rows = dest_edge < 2
        to_rows = jnp.logical_and(
            outer, jnp.logical_and(dest_rows, dest_edge == jnp.where(r == 0, 0, 1))
        )
        to_cols = jnp.logical_not(dest_rows)
        block = dest_group * 8 + jnp.where(dest_edge == 2, 0, 7)
        lower = jnp.where(r == 15, 5, 0)
        line = spots((48, 80), 0) - lower

        @pl.when(edge < 2)
        def _():
            @pl.when(to_cols)
            def _():
                moved = place(chunks[edge], face, dest_face)
                q = 64 * c + spots((48, 80), 1) - 8
                p = jnp.where(turned == 1, 511 - q, q)
                pick = one_hot(jnp.logical_and(p - 32 * r + 8 == line, line >= 3))
                out[block, 64:112, :] += dot(pick, moved).astype(BF16)

            @pl.when(to_rows)
            def _():
                moved = place(chunks[edge], face, dest_face)
                q = 64 * c + spots((80, 80), 1) - 8
                p = jnp.where(turned == 1, 511 - q, q)
                middle = jnp.where(turned == 1, 7 - c, c)
                for shift in (-1, 0, 1):
                    target = middle + shift

                    @pl.when(jnp.logical_and(target >= 0, target < 8))
                    def _():
                        lead = jnp.where(target == 0, 0, 8)
                        seen = p - 64 * target + lead
                        kept = seen < jnp.where(target == 0, 72, 80)
                        pick = one_hot(jnp.logical_and(kept, seen == spots((80, 80), 0)))
                        out[dest_group * 8 + target, 0:80, :] += dot(pick, moved).astype(BF16)

        @pl.when(jnp.logical_and(edge >= 2, c == jnp.where(edge == 2, 0, 7)))
        def _():
            @pl.when(to_cols)
            def _():
                start = pl.multiple_of(32 * jnp.where(turned == 1, 15 - r, r), 8)
                moved = place(strip[pl.ds(start, 48), :], face, dest_face)
                x = spots((48, 48), 1)
                line = spots((48, 48), 0) - lower
                pick = one_hot(jnp.logical_and(jnp.where(turned == 1, 47 - x, x) == line, line >= 3))
                out[block, 64:112, :] += dot(pick, moved).astype(BF16)

            @pl.when(to_rows)
            def _():
                x = spots((80, 80), 1)
                pick = one_hot(jnp.where(turned == 1, 79 - x, x) == spots((80, 80), 0))
                for target in range(8):
                    start = pl.multiple_of(
                        jnp.where(turned == 1, 448 - 64 * target, 64 * target), 8
                    )
                    moved = place(strip[pl.ds(start, 80), :], face, dest_face)
                    chosen = dot(pick, moved)
                    if target == 0:
                        chosen = jnp.concatenate([chosen[8:], jnp.zeros((8, 256), F32)], axis=0)
                    out[dest_group * 8 + target, 0:80, :] += chosen.astype(BF16)

        return carry

    lax.fori_loop(0, 12, one_strip, 0)

    @pl.when(jnp.logical_and(outer, side))
    def _():
        def one_run(k, carry):
            face, kind = k >> 2, k & 3
            edge = jnp.where(kind < 2, kind, jnp.where(c == 0, 2, 3))
            end = jnp.where(kind < 2, jnp.where(c == 0, 0, 1), kind & 1)
            first = ((3 * g + face) * 4 + edge) * 3
            between, across = nb[first], nb[first + 1]
            far = jnp.where(nb[first + 2] == 1, 1 - end, end)
            second = (between * 4 + jnp.where(across < 2, 2 + far, far)) * 3
            dest, dest_edge = nb[second], nb[second + 1]
            near = across & 1
            near = jnp.where(nb[second + 2] == 1, 1 - near, near)
            dest_group = third(dest)
            slot = dest - 3 * dest_group + jnp.where(dest_edge < 2, 0, 3)
            dest_row = jnp.where(dest_edge < 2, dest_edge, near)
            dest_col = jnp.where(dest_edge < 2, near, dest_edge - 2)

            @pl.when(dest_row == jnp.where(r == 0, 0, 1))
            def _():
                at_chunk = pl.multiple_of(jnp.where(end == 1, 64, 8), 8)
                at_strip = pl.multiple_of(jnp.where(end == 1, 512, 8), 8)
                data = jnp.where(
                    edge < 2,
                    chunks[jnp.minimum(edge, 1), pl.ds(at_chunk, 8), :],
                    strip[pl.ds(at_strip, 8), :],
                )
                data = pltpu.roll(data, 240 - 80 * face, 1)[:, 128:256]
                data = jnp.where(spots((8, 128), 1) >= 112, data, 0.0)
                data = jnp.concatenate([data, jnp.zeros((8, 128), F32)], axis=0).astype(BF16)
                row = pl.multiple_of(16 * slot, 16)
                out[dest_group * 8 + 7 * dest_col, pl.ds(row, 16), 128:256] += data

            return carry

        lax.fori_loop(0, 12, one_run, 0)

    copy = pltpu.make_async_copy(out, target, sem)
    copy.start()
    copy.wait()


def normalise(mixed, gain):
    center = jnp.mean(mixed, axis=-1, keepdims=True)
    apart = mixed - center
    spread = jnp.mean(apart * apart, axis=-1, keepdims=True)
    return (apart * lax.rsqrt(spread + EPSILON) * gain).astype(BF16)


def rounded(x):
    return x.astype(BF16).astype(F32)


def fetch(sources, targets, sems):
    copies = [
        pltpu.make_async_copy(a, b, sems.at[k]) for k, (a, b) in enumerate(zip(sources, targets))
    ]
    for copy in copies:
        copy.start()
    return copies


def spread(index, above, fields, below, before, after, cells):
    cells[0, 8:40, :] = before[index].astype(F32)
    cells[9, 8:40, :] = after[index].astype(F32)
    for k in range(8):
        cells[1 + k, 8:40, :] = fields[index, :, 128 * k : 128 * k + 128].astype(F32)
    for k in range(10):
        cells[k, 0:8, :] = above[index, :, 128 * k : 128 * k + 128].astype(F32)
        cells[k, 40:48, :] = below[index, :, 128 * k : 128 * k + 128].astype(F32)


def bulk_kernel(
    pos, fields, above, below, before, after, enc_cells,
    kernel_first, gain_first, expand_first, bias_first, contract_first, scale_first, down,
    kernel_second, gain_second, expand_second, bias_second, contract_second, scale_second,
    out, edge_rows, edge_cols,
    cells, grid, rows, pooled, coarse, result, *rest,
):
    r, c = pos[1], pos[2]
    sources = (
        fields, above, below, before, after, enc_cells,
        kernel_first, gain_first, expand_first, bias_first, contract_first, scale_first, down,
        kernel_second, gain_second, expand_second, bias_second, contract_second, scale_second,
    )
    held, sems, leave = rest[:-2], rest[-2], rest[-1]
    copies = fetch(sources, held, sems)
    (
        fields, above, below, before, after, enc_cells,
        kernel_first, gain_first, expand_first, bias_first, contract_first, scale_first, down,
        kernel_second, gain_second, expand_second, bias_second, contract_second, scale_second,
    ) = held
    for copy in copies[:6]:
        copy.wait()

    def encode(i, carry):
        spread(i, above, fields, below, before, after, cells)
        stacked = cells[...].reshape(480, 128).astype(BF16)
        for n in range(4):
            product = rounded(dot(stacked, enc_cells[:, 256 * n : 256 * n + 256]))
            for k in range(10):
                for j in range(2):
                    line = product[48 * k : 48 * k + 48, 128 * j : 128 * j + 128]
                    grid[80 * i + 8 * k + 2 * n + j] = line
        return carry

    lax.fori_loop(0, 3, encode, 0)
    for copy in copies[6:13]:
        copy.wait()

    def one_face(i, carry):
        def one_chunk(k, carry):
            j0 = 80 * i + 4 + 24 * k
            total = jnp.zeros((24, 40, 128), F32)
            for a in range(3):
                for b in range(3):
                    window = grid[pl.ds(j0 + b - 1, 24), 3 + a : 43 + a, :]
                    total = total + window * kernel_first[3 * a + b : 3 * a + b + 1, :][None]
            normed = normalise(total.reshape(960, C1), gain_first[...])
            hidden = gelu(dot(normed, expand_first[...]) + bias_first[...]).astype(BF16)
            update = dot(hidden, contract_first[...])
            here = grid[pl.ds(j0, 24), 4:44, :].reshape(960, C1)
            rows[...] = rounded(here + scale_first[...] * update).reshape(24, 40, C1)
            paired = rows[:, pl.ds(0, 20, stride=2), :] + rows[:, pl.ds(1, 20, stride=2), :]
            paired = paired.reshape(12, 2, 20, C1)
            pooled[pl.ds(12 * k, 12), 0:20, :] = 0.25 * (paired[:, 0] + paired[:, 1])
            return carry

        lax.fori_loop(0, 3, one_chunk, 0, unroll=3)
        pooled[:, 20:24, :] = jnp.zeros((36, 4, C1), F32)
        product = dot(pooled[...].reshape(36 * 24, C1).astype(BF16), down[...])
        coarse[i] = rounded(product).reshape(36, 24, C2)
        return carry

    lax.fori_loop(0, 3, one_face, 0)
    for copy in copies[13:]:
        copy.wait()

    def at_edges(act):
        for index, (at, source, target) in enumerate(
            (
                (r == 0, coarse.at[:, :, 0:8], edge_rows),
                (r == 15, coarse.at[:, :, 12:20], edge_rows),
                (c == 0, coarse.at[:, 0:7], edge_cols),
                (c == 7, coarse.at[:, 29:36], edge_cols),
            )
        ):

            @pl.when(at)
            def _():
                act(pltpu.make_async_copy(source, target, leave.at[3 + index]))

    at_edges(lambda copy: copy.start())

    def one_part(k, carry):
        i, part = k >> 1, k & 1
        first = 16 * part
        total = jnp.zeros((16, 16, C2), F32)
        for a in range(3):
            for b in range(3):
                window = coarse[i, pl.ds(first + 2 * b, 16), 2 * a : 2 * a + 16, :]
                total = total + window * kernel_second[3 * a + b : 3 * a + b + 1, :][None]
        normed = normalise(total.reshape(256, C2), gain_second[...])
        hidden = gelu(dot(normed, expand_second[...]) + bias_second[...]).astype(BF16)
        update = dot(hidden, contract_second[...])
        here = coarse[i, pl.ds(first + 2, 16), 2:18, :].reshape(256, C2)
        made = (here + scale_second[...] * update).astype(BF16).reshape(16, 16, C2)
        for j in range(16):
            lane = pl.multiple_of((first + j) * C2, C2)
            result[i, :, pl.ds(lane, C2)] = made[j]
        return carry

    for i in range(3):
        lax.fori_loop(2 * i, 2 * i + 2, one_part, 0, unroll=2)
        pltpu.make_async_copy(result.at[i], out.at[i], leave.at[i]).start()
    for i in range(3):
        pltpu.make_async_copy(result.at[i], out.at[i], leave.at[i]).wait()
    at_edges(lambda copy: copy.wait())


def edge_kernel(
    nb, pos, bands, fields, above, below, before, after, first_out, edge_rows, edge_cols, enc_cells,
    kernel_first, gain_first, expand_first, bias_first, contract_first, scale_first, down,
    kernel_second, gain_second, expand_second, bias_second, contract_second, scale_second,
    out, *scratch,
):
    r, c = pos[1], pos[2]
    either = jnp.logical_or(
        jnp.logical_or(r == 0, r == 15), jnp.logical_or(c == 0, c == 7)
    )
    held, sems = scratch[-23:-1], scratch[-1]
    sources = (
        enc_cells, fields, above, below, before, after,
        kernel_first, gain_first, expand_first, bias_first, contract_first, scale_first, down,
        kernel_second, edge_rows, edge_cols, gain_second, expand_second, bias_second,
        contract_second, scale_second, first_out,
    )

    @pl.when(either)
    def _():
        copies = fetch(sources, held, sems)
        patched(nb, pos, bands, held, copies, out, sems, *scratch[:-23])


def patched(
    nb, pos, bands, held, copies, out, sems,
    cells, grid, side_grid, banded, taps, side_taps, mix, strip, rows, pooled, side_pooled,
    level, side_level, mixed, center, packed, patch,
):
    (
        enc_cells, fields, above, below, before, after,
        kernel_first, gain_first, expand_first, bias_first, contract_first, scale_first, down,
        kernel_second, edge_rows, edge_cols, gain_second, expand_second, bias_second,
        contract_second, scale_second, result,
    ) = held
    g, r, c = pos[0], pos[1], pos[2]
    top, bottom, left, right = r == 0, r == 15, c == 0, c == 7
    outer = jnp.logical_or(top, bottom)
    side = jnp.logical_or(left, right)
    corner = jnp.logical_and(outer, side)
    edge_row, edge_col = jnp.where(top, 0, 1), jnp.where(left, 2, 3)

    def add(k, total):
        return total + bands[k]

    total = lax.fori_loop(0, 32, add, jnp.zeros((112, 256), BF16), unroll=8)
    both = jnp.concatenate([total[:, 0:128], total[:, 128:256]], axis=0)
    copies[0].wait()
    for k in range(4):
        product = rounded(dot(both, enc_cells[:, 256 * k : 256 * k + 256]))
        for j in range(2):
            banded[2 * k + j, 0:112, :] = product[0:112, 128 * j : 128 * j + 128]
            banded[8 + 2 * k + j, 0:112, :] = product[112:224, 128 * j : 128 * j + 128]
    banded[:, 112:120, :] = jnp.zeros((16, 8, 128), F32)
    none = jnp.zeros((8, 128), F32)

    def row_band(k):
        body = banded[k, 0:80, :]
        shifted = jnp.concatenate([none, body[0:72]], axis=0)
        return jnp.where(left, shifted, jnp.concatenate([body[0:72], jnp.where(right, none, body[72:80])], axis=0))

    def row_band_end(k):
        at_left = jnp.concatenate([none, banded[k, 0:8, :]], axis=0)
        return jnp.where(left, at_left, jnp.concatenate([banded[k, 64:72, :], none], axis=0))

    def col_band(k):
        return jnp.where(bottom, banded[k, 69:117, :], banded[k, 64:112, :])

    def band_tap(face, edge, a, b):
        base = ((3 * g + face) * 4 + edge) * 3
        other_edge, turned = nb[base + 1], nb[base + 2]
        down_row, down_col = a - 1, b - 1
        deep = jnp.where(
            edge == 0,
            -down_row,
            jnp.where(edge == 1, down_row, jnp.where(edge == 2, -down_col, down_col)),
        )
        along = jnp.where(edge < 2, down_col, down_row)
        along = jnp.where(turned == 1, -along, along)
        inward = jnp.where((other_edge & 1) == 0, deep, -deep)
        tap_row = jnp.where(other_edge < 2, inward, along)
        tap_col = jnp.where(other_edge < 2, along, inward)
        return kernel_first[pl.ds((tap_row + 1) * 3 + tap_col + 1, 1), :]

    def run_end(face, edge, end):
        first = ((3 * g + face) * 4 + edge) * 3
        far = jnp.where(nb[first + 2] == 1, 1 - end, end)
        across = jnp.where(nb[first + 1] < 2, 2 + far, far)
        near = nb[first + 1] & 1
        return jnp.where(nb[(nb[first] * 4 + across) * 3 + 2] == 1, 1 - near, near)

    def block_first(total, here):
        normed = normalise(total, gain_first[...])
        hidden = gelu(dot(normed, expand_first[...]) + bias_first[...]).astype(BF16)
        return rounded(here + scale_first[...] * dot(hidden, contract_first[...]))

    for copy in copies[1:13]:
        copy.wait()
    for i in range(3):
        spread(i, above, fields, below, before, after, cells.at[i])

    @pl.when(outer)
    def _():
        low = pl.multiple_of(jnp.where(top, 0, 32), 8)
        data = cells[:, :, pl.ds(low, 16), :].reshape(480, 128).astype(BF16)
        for n in range(4):
            product = rounded(dot(data, enc_cells[:, 256 * n : 256 * n + 256]))
            for i in range(3):
                for k in range(10):
                    for j in range(2):
                        row = 160 * i + 16 * k
                        line = product[row : row + 16, 128 * j : 128 * j + 128]
                        grid[80 * i + 8 * k + 2 * n + j] = line
        flat = grid.reshape(3840, 128)
        for at, first, step in ((top, 7, -1), (bottom, 8, 1)):

            @pl.when(at)
            def _():
                for i in range(3):
                    for k in range(DEPTH):
                        line = row_band(5 * i + k)
                        flat[pl.ds(1280 * i + first + step * k, 80, stride=16), :] = line

        for a in range(3):
            for b in range(3):
                own = jnp.broadcast_to(kernel_first[3 * a + b : 3 * a + b + 1, :], (4, 128))
                for i in range(3):
                    line = jnp.broadcast_to(band_tap(i, edge_row, a, b), (4, 128))
                    taps[9 * i + 3 * a + b, 0:4, :] = jnp.where(top, line, own)
                    taps[9 * i + 3 * a + b, 4:8, :] = jnp.where(top, own, line)

        def one_chunk(k, carry):
            i = k
            j0 = 80 * i + 4
            total = jnp.zeros((72, 8, 128), F32)
            for a in range(3):
                for b in range(3):
                    window = grid[pl.ds(j0 + b - 1, 72), 3 + a : 11 + a, :]
                    total = total + window * taps[9 * i + 3 * a + b][None]
            here = grid[pl.ds(j0, 72), 4:12, :].reshape(576, C1)
            slot = lax.rem(k, 3)
            strip[slot] = block_first(total.reshape(576, C1), here).reshape(72, 8, C1)
            paired = strip[slot, :, pl.ds(0, 4, stride=2), :] + strip[slot, :, pl.ds(1, 4, stride=2), :]
            paired = paired.reshape(36, 2, 4, C1)
            pooled[pl.ds(36 * k, 36), 0:4, :] = 0.25 * (paired[:, 0] + paired[:, 1])
            return carry

        pooled[...] = jnp.zeros_like(pooled)
        lax.fori_loop(0, 3, one_chunk, 0, unroll=3)
    for copy in copies[13:16]:
        copy.wait()

    @pl.when(outer)
    def _():
        product = rounded(dot(pooled[...].reshape(864, C1).astype(BF16), down[...]))
        product = product.reshape(108, 8, C2)
        whole = edge_rows[...].reshape(108, 8, C2)
        level[...] = jnp.where(top, whole, jnp.concatenate([whole[:, 1:], whole[:, :1]], axis=1))

        @pl.when(top)
        def _():
            level[:, 0:4, :] = product[:, 0:4]

        @pl.when(bottom)
        def _():
            level[:, 3:7, :] = product[:, 0:4]

    @pl.when(side)
    def _():
        group = jnp.where(left, 0, 8)
        data = cells[:, pl.ds(group, 2)].reshape(288, 128).astype(BF16)
        for n in range(4):
            product = rounded(dot(data, enc_cells[:, 256 * n : 256 * n + 256]))
            for i in range(3):
                for k in range(2):
                    for j in range(2):
                        row = 96 * i + 48 * k
                        line = product[row : row + 48, 128 * j : 128 * j + 128]
                        side_grid[16 * i + 8 * k + 2 * n + j] = line
        for i in range(3):
            for k in range(DEPTH):
                j = jnp.where(left, 7 - k, 8 + k)
                side_grid[16 * i + j] = col_band(5 * i + k)

        flat = side_grid.reshape(2304, 128)
        for at, first, step in ((top, 7, -1), (bottom, 40, 1)):

            @pl.when(at)
            def _():
                for i in range(3):
                    for k in range(DEPTH):
                        line = row_band_end(5 * i + k)
                        flat[pl.ds(768 * i + first + step * k, 16, stride=48), :] = line

        inner = jnp.where(left, 1, 0)
        for a in range(3):
            for b in range(3):
                own = jnp.broadcast_to(kernel_first[3 * a + b : 3 * a + b + 1, :], (40, 128))
                for i in range(3):
                    line = jnp.broadcast_to(band_tap(i, edge_col, a, b), (40, 128))
                    side_taps[i, inner, 3 * a + b] = own
                    side_taps[i, 1 - inner, 3 * a + b] = line

        for at, row in ((top, 0), (bottom, 36)):

            @pl.when(at)
            def _():
                for a in range(3):
                    for b in range(3):
                        for i in range(3):
                            line = jnp.broadcast_to(band_tap(i, edge_row, a, b), (4, 128))
                            side_taps[i, inner, 3 * a + b, row : row + 4, :] = line

        for i in range(3):
            for half in range(2):
                total = jnp.zeros((4, 40, 128), F32)
                for a in range(3):
                    for b in range(3):
                        j = 16 * i + 3 + 4 * half + b
                        window = side_grid[j : j + 4, 3 + a : 43 + a, :]
                        total = total + window * side_taps[i, half, 3 * a + b][None]
                mix[i, 4 * half : 4 * half + 4] = total

        @pl.when(corner)
        def _():
            out_a, out_b = jnp.where(top, 0, 2), jnp.where(left, 0, 2)
            row_in, row_out = jnp.where(top, 8, 39), jnp.where(top, 7, 40)
            col_in, col_out = jnp.where(left, 8, 7), jnp.where(left, 7, 8)
            step_row, step_col = jnp.where(top, -1, 1), jnp.where(left, -1, 1)
            for i in range(3):
                row_end = run_end(i, edge_row, jnp.where(left, 0, 1))
                col_end = run_end(i, edge_col, jnp.where(top, 0, 1))
                row_lines = [-side_grid[16 * i + col_out, pl.ds(row_in, 1), :]] + [
                    banded[15, pl.ds(16 * i + jnp.where(row_end == 1, 7 - d, d), 1), :]
                    for d in range(DEPTH)
                ]
                col_lines = [-side_grid[16 * i + col_in, pl.ds(row_out, 1), :]] + [
                    banded[15, pl.ds(48 + 16 * i + jnp.where(col_end == 1, 7 - d, d), 1), :]
                    for d in range(DEPTH)
                ]
                row_taps = [band_tap(i, edge_row, 1 + s * step_row, out_b) for s in (-1, 0, 1)]
                col_taps = [band_tap(i, edge_col, out_a, 1 + s * step_col) for s in (-1, 0, 1)]
                for depth in range(4):
                    extra = sum(row_taps[s] * row_lines[depth + s] for s in range(3))
                    at = (i, col_in - 4, pl.ds(row_out + depth * step_row - 4, 1))
                    mix[at[0], at[1], at[2], :] += extra
                    extra = sum(col_taps[s] * col_lines[depth + s] for s in range(3))
                    at = (i, col_out + depth * step_col - 4, pl.ds(row_in - 4, 1))
                    mix[at[0], at[1], at[2], :] += extra

        side_pooled[...] = jnp.zeros_like(side_pooled)
        for i in range(3):
            here = side_grid[16 * i + 4 : 16 * i + 12, 4:44, :].reshape(320, C1)
            rows[i] = block_first(mix[i].reshape(320, C1), here).reshape(8, 40, C1)
            paired = rows[i, :, pl.ds(0, 20, stride=2), :] + rows[i, :, pl.ds(1, 20, stride=2), :]
            paired = paired.reshape(4, 2, 20, C1)
            side_pooled[4 * i : 4 * i + 4, 0:20, :] = 0.25 * (paired[:, 0] + paired[:, 1])
        product = rounded(dot(side_pooled[...].reshape(288, C1).astype(BF16), down[...]))
        product = product.reshape(12, 24, C2)
        side_level[...] = edge_cols[...].reshape(21, 24, C2)
        first = jnp.where(left, 0, 29)

        @pl.when(top)
        def _():
            for i in range(3):
                for k in range(7):
                    side_level[7 * i + k, 0:4, :] = level[36 * i + first + k, 0:4, :]

        @pl.when(bottom)
        def _():
            for i in range(3):
                for k in range(7):
                    side_level[7 * i + k, 16:20, :] = level[36 * i + first + k, 3:7, :]

        shift = jnp.where(left, 0, 3)
        dead = jnp.where(left, 0, 5)
        for i in range(3):
            for k in range(4):
                side_level[7 * i + shift + k] = product[4 * i + k]

        for at, row, low in ((top, 0, 0), (bottom, 18, 13)):

            @pl.when(at)
            def _():
                for i in range(3):
                    for k in range(2):
                        side_level[7 * i + dead + k, row : row + 2, :] = jnp.zeros((2, C2), F32)
                    for k in range(7):
                        line = side_level[7 * i + k, low : low + 7, :]
                        level[36 * i + first + k, 0:7, :] = line

    mixed[...] = jnp.zeros_like(mixed)
    center[...] = jnp.zeros_like(center)

    @pl.when(outer)
    def _():
        for i in range(3):
            total = jnp.zeros((32, 3, C2), F32)
            for a in range(3):
                for b in range(3):
                    first = 36 * i + 2 * b
                    window = level[first : first + 32, 2 * a : 2 * a + 3, :]
                    total = total + window * kernel_second[3 * a + b : 3 * a + b + 1, :][None]
            here = level[36 * i + 2 : 36 * i + 34, 2:5, :]
            for j in range(32):
                row = 96 * i + 3 * j
                mixed[row : row + 3, :] = total[j]
                center[row : row + 3, :] = here[j]

    @pl.when(side)
    def _():
        for i in range(3):
            total = jnp.zeros((3, 16, C2), F32)
            for a in range(3):
                for b in range(3):
                    first = 7 * i + 2 * b
                    window = side_level[first : first + 3, 2 * a : 2 * a + 16, :]
                    total = total + window * kernel_second[3 * a + b : 3 * a + b + 1, :][None]
            row = 288 + 48 * i
            mixed[row : row + 48, :] = total.reshape(48, C2)
            center[row : row + 48, :] = side_level[7 * i + 2 : 7 * i + 5, 2:18, :].reshape(48, C2)

    for copy in copies[16:]:
        copy.wait()
    normed = normalise(mixed[...], gain_second[...])
    hidden = gelu(dot(normed, expand_second[...]) + bias_second[...]).astype(BF16)
    center[...] = center[...] + scale_second[...] * dot(hidden, contract_second[...])

    for i in range(3):
        for at, row in ((top, 0), (bottom, 13)):

            @pl.when(at)
            def _():
                patch[...] = result[i].astype(F32)
                for j in range(32):
                    line = center[96 * i + 3 * j : 96 * i + 3 * j + 3, :]
                    patch[row : row + 3, C2 * j : C2 * j + C2] = line
                result[i] = patch[...].astype(BF16)

        for at, col in ((left, 0), (right, 29)):

            @pl.when(at)
            def _():
                for j in range(3):
                    row = 288 + 48 * i + 16 * j
                    lane = C2 * (col + j)
                    result[i, :, lane : lane + C2] = center[row : row + 16, :].astype(BF16)

        pltpu.make_async_copy(result.at[i], out.at[i], sems.at[i]).start()
    for i in range(3):
        pltpu.make_async_copy(result.at[i], out.at[i], sems.at[i]).wait()


SMEM = pl.BlockSpec(memory_space=pltpu.SMEM)
WHOLE = pl.BlockSpec(memory_space=pltpu.VMEM)
FAR = pl.BlockSpec(memory_space=pltpu.HBM)

LIMIT = 56 * 2**20


def held_copies(weights):
    held = [pltpu.VMEM(w.shape, w.dtype) for w in weights]
    return held + [pltpu.SemaphoreType.DMA((len(weights),))]


def strips(pos, fields):
    return pl.pallas_call(
        strip_kernel,
        out_shape=(
            jax.ShapeDtypeStruct((16, 48, 256), BF16),
            jax.ShapeDtypeStruct((64, 256), BF16),
        ),
        in_specs=[SMEM, WHOLE],
        out_specs=(WHOLE, WHOLE),
        compiler_params=pltpu.CompilerParams(vmem_limit_bytes=24 * 2**20),
        name="strips",
    )(pos, fields)


def route(links, pos, recv, lines, opposite):
    return pl.pallas_call(
        route_kernel,
        out_shape=jax.ShapeDtypeStruct((32, 112, 256), BF16),
        in_specs=[SMEM, SMEM, WHOLE, WHOLE, WHOLE],
        out_specs=FAR,
        scratch_shapes=[
            pltpu.VMEM((2, 80, 256), F32),
            pltpu.VMEM((528, 256), F32),
            pltpu.VMEM((32, 112, 256), BF16),
            pltpu.SemaphoreType.DMA,
        ],
        compiler_params=pltpu.CompilerParams(vmem_limit_bytes=16 * 2**20),
        cost_estimate=pl.CostEstimate(
            flops=10**9, bytes_accessed=4 * 10**6, transcendentals=0
        ),
        name="route",
    )(links, pos, recv, lines, opposite)


def bulk(pos, halos, enc_cells, weights):
    operands = (*halos, enc_cells, *weights)
    return pl.pallas_call(
        bulk_kernel,
        out_shape=(
            jax.ShapeDtypeStruct((3, 16, 32 * C2), BF16),
            jax.ShapeDtypeStruct((3, 36, 8, C2), F32),
            jax.ShapeDtypeStruct((3, 7, 24, C2), F32),
        ),
        in_specs=[SMEM] + [FAR] * len(operands),
        out_specs=(FAR, FAR, FAR),
        scratch_shapes=[
            pltpu.VMEM((10, 48, 128), F32),
            pltpu.VMEM((240, 48, 128), F32),
            pltpu.VMEM((24, 40, 128), F32),
            pltpu.VMEM((36, 24, 128), F32),
            pltpu.VMEM((3, 36, 24, 256), F32),
            pltpu.VMEM((3, 16, 32 * C2), BF16),
        ]
        + held_copies(operands)
        + [pltpu.SemaphoreType.DMA((7,))],
        compiler_params=pltpu.CompilerParams(vmem_limit_bytes=LIMIT),
        cost_estimate=pl.CostEstimate(
            flops=5 * 10**9, bytes_accessed=4 * 10**6, transcendentals=6 * 10**6
        ),
        name="bulk",
    )(pos, *operands)


def edges(links, pos, halos, bands, first_out, edge_rows, edge_cols, enc_cells, weights):
    sources = (enc_cells, *halos, *weights[:8], edge_rows, edge_cols, *weights[8:], first_out)
    operands = (bands, *halos, first_out, edge_rows, edge_cols, enc_cells, *weights)
    return pl.pallas_call(
        edge_kernel,
        out_shape=jax.ShapeDtypeStruct((3, 16, 32 * C2), BF16),
        in_specs=[SMEM, SMEM, WHOLE] + [FAR] * (len(operands) - 1),
        out_specs=FAR,
        input_output_aliases={2 + len(halos) + 1: 0},
        scratch_shapes=[
            pltpu.VMEM((3, 10, 48, 128), F32),
            pltpu.VMEM((240, 16, 128), F32),
            pltpu.VMEM((48, 48, 128), F32),
            pltpu.VMEM((16, 120, 128), F32),
            pltpu.VMEM((27, 8, 128), F32),
            pltpu.VMEM((3, 2, 9, 40, 128), F32),
            pltpu.VMEM((3, 8, 40, 128), F32),
            pltpu.VMEM((3, 72, 8, 128), F32),
            pltpu.VMEM((3, 8, 40, 128), F32),
            pltpu.VMEM((108, 8, 128), F32),
            pltpu.VMEM((12, 24, 128), F32),
            pltpu.VMEM((108, 8, 256), F32),
            pltpu.VMEM((21, 24, 256), F32),
            pltpu.VMEM((432, 256), F32),
            pltpu.VMEM((432, 256), F32),
            pltpu.VMEM((8, 128), F32),
            pltpu.VMEM((16, 32 * C2), F32),
        ]
        + held_copies(sources),
        compiler_params=pltpu.CompilerParams(vmem_limit_bytes=LIMIT),
        name="edges",
    )(links, pos, *operands)


def per_device(
    fields,
    neighbours,
    w_enc,
    depthwise_kernel_first,
    norm_gain_first,
    expand_weight_first,
    expand_bias_first,
    contract_weight_first,
    layer_scale_first,
    w_down,
    depthwise_kernel_second,
    norm_gain_second,
    expand_weight_second,
    expand_bias_second,
    contract_weight_second,
    layer_scale_second,
):
    r, c = lax.axis_index("row"), lax.axis_index("col")
    pos = jnp.stack([lax.axis_index("face"), r, c]).astype(jnp.int32)
    links = neighbours.reshape(144)

    send, lines = strips(pos, fields)
    recv = lax.all_to_all(send, "row", 0, 0)
    opposite = lax.ppermute(lines, "row", [(0, 15), (15, 0)])

    before = lax.ppermute(fields[:, :, 896:], "col", [(k, k + 1) for k in range(7)])
    after = lax.ppermute(fields[:, :, :128], "col", [(k + 1, k) for k in range(7)])
    wide = jnp.concatenate([before, fields, after], axis=2)
    above = lax.ppermute(wide[:, 24:], "row", [(k, k + 1) for k in range(15)])
    below = lax.ppermute(wide[:, :8], "row", [(k + 1, k) for k in range(15)])

    routed = route(links, pos, recv, lines, opposite)
    routed, above, below = lax.optimization_barrier((routed, above, below))
    bands = lax.all_to_all(routed, ("face", "col"), 0, 0)

    enc_cells = jnp.kron(jnp.eye(8, dtype=BF16), w_enc)
    weights = (
        depthwise_kernel_first.reshape(9, C1),
        norm_gain_first.reshape(1, C1),
        expand_weight_first,
        expand_bias_first.reshape(1, HID1),
        contract_weight_first,
        layer_scale_first.reshape(1, C1),
        w_down,
        depthwise_kernel_second.reshape(9, C2),
        norm_gain_second.reshape(1, C2),
        expand_weight_second,
        expand_bias_second.reshape(1, HID2),
        contract_weight_second,
        layer_scale_second.reshape(1, C2),
    )
    halos = (fields, above, below, before, after)
    first_out, edge_rows, edge_cols = bulk(pos, halos, enc_cells, weights)
    return edges(links, pos, halos, bands, first_out, edge_rows, edge_cols, enc_cells, weights)


def solution(mesh):
    return jax.shard_map(
        per_device,
        mesh=mesh,
        in_specs=(P("face", "row", "col"),) + (P(),) * 15,
        out_specs=P("face", "row", "col"),
        check_vma=False,
    )
```
